256 devices in a mesh: dp: 4 (over x), ctx: 16 (over z, core), head: 4 (over y).
Axes of the slice: x: 4, y: 4, z: 8, core: 2. Of those that a mesh axis runs over, the one named last changes fastest.
Arguments:
- inputs: bfloat16 [4, 2048, 4096], P('dp', 'ctx', 'head'), may hold values from -6 to 6
- step_rate: float32 [4, 2048, 4096], P('dp', 'ctx', 'head'), may hold values from 0 to 12
- key_rows: bfloat16 [4, 2048, 16], P('dp', 'ctx'), may hold values from -5 to 5
- query_rows: bfloat16 [4, 2048, 16], P('dp', 'ctx'), may hold values from -1.5 to 1.5
- grad_out: bfloat16 [4, 2048, 4096], P('dp', 'ctx', 'head'), may hold values from -6 to 6
Outputs:
- grad_inputs: bfloat16 [4, 2048, 4096], P('dp', ('ctx', 'head'))
- grad_rate: bfloat16 [4, 2048, 4096], P('dp', ('ctx', 'head'))
- grad_keys: float32 [4, 2048, 16], P('dp', ('ctx', 'head'))
- grad_queries: float32 [4, 2048, 16], P('dp', ('ctx', 'head'))
The draws below stay inside these ranges and needn't reach their ends.
All inputs are finite; a program needn't handle non-finite values.
Results may differ from the reference program's by a relative error of at most 0.0018.
Values may be sent and summed in bfloat16 or wider, within the bound.
A program may use at most 64 MiB of HBM per device.

```python
import math
import jax
import jax.numpy as jnp
from jax import lax

INNER = 4096
STATE = 16
BLOCK = 16
SEQUENCE_COUNT = 4
SEQUENCE_LENGTH = 2048


def draw_step_rate(key, part):
    key = jax.random.fold_in(key, 7)
    every_key = jax.random.split(key, 7)
    shape_ch = (SEQUENCE_COUNT, 1, INNER)
    rate_logarithm = jax.random.uniform(every_key[0], shape_ch, jnp.float32, math.log(3e-05), math.log(0.08))
    positions = jnp.arange(SEQUENCE_LENGTH, dtype=jnp.float32)[None, :, None]
    phase = jax.random.uniform(every_key[3], (SEQUENCE_COUNT, 1, 1), jnp.float32, 0.0, 2.0 * math.pi)
    steady_input = jnp.exp(0.7 * jnp.sin(6.0 * math.pi * positions / SEQUENCE_LENGTH + phase))
    noisy_input = jnp.exp(jax.random.uniform(every_key[4], (SEQUENCE_COUNT, SEQUENCE_LENGTH, INNER), jnp.float32, -0.7, 0.7))
    spike_mask = jax.random.bernoulli(every_key[5], 8.0 / SEQUENCE_LENGTH, (SEQUENCE_COUNT, SEQUENCE_LENGTH, 1))
    spike_value = jax.random.uniform(every_key[6], (SEQUENCE_COUNT, SEQUENCE_LENGTH, 1), jnp.float32, 4.0, 12.0)
    rate_values = jnp.where(spike_mask, spike_value, jnp.exp(rate_logarithm) * steady_input * noisy_input)
    return rate_values.astype(jnp.float32)


def block_levels(stream_key, extent, pieces, least, top_value):
    def one(dim, shards_of):
        draws = jax.random.uniform(jax.random.fold_in(jax.random.fold_in(stream_key, 6), dim), (shards_of,), jnp.float32, least / len(pieces), top_value / len(pieces))
        return jnp.repeat(jnp.exp(draws), extent[dim] // shards_of).reshape((-1,) + (1,) * (len(extent) - dim - 1))

    level = one(*pieces[0])
    for cut in pieces[1:]:
        level = level * one(*cut)
    return level


def normal_values(key, extent, width, limit, cuts=(), held_as=jnp.bfloat16):
    drawn = width * jax.random.normal(key, extent, jnp.float32)
    if cuts:
        drawn = drawn * block_levels(key, extent, cuts, -0.22, 0.18)
    return jnp.clip(drawn, -limit, limit).astype(held_as)


def setup_inputs(seed: int = 0) -> dict:
    arg_keys = jax.random.split(jax.random.key(seed), 6)
    return {
        "inputs": normal_values(arg_keys[0], (SEQUENCE_COUNT, SEQUENCE_LENGTH, INNER), 1.0, 6.0, ((0, 4), (1, 16), (2, 4))),
        "step_rate": draw_step_rate(jax.random.fold_in(arg_keys[5], 71), 0),
        "key_rows": normal_values(arg_keys[2], (SEQUENCE_COUNT, SEQUENCE_LENGTH, STATE), 1.0, 5.0, ((0, 4), (1, 16))),
        "query_rows": normal_values(arg_keys[3], (SEQUENCE_COUNT, SEQUENCE_LENGTH, STATE), STATE ** -0.5, 1.5, ((0, 4), (1, 16))),
        "grad_out": normal_values(arg_keys[4], (SEQUENCE_COUNT, SEQUENCE_LENGTH, INNER), 1.0, 6.0, ((0, 4), (1, 16), (2, 4))),
    }


def affine(earlier, subsequent):
    return (earlier[0] * subsequent[0], subsequent[0] * earlier[1] + subsequent[1])


def block_setup(inputs, rate_values, key_blk):
    keys_sq = key_blk * key_blk
    key_norm = jnp.sum(keys_sq, axis=1)
    denominator = 1.0 + rate_values * key_norm[:, None]
    step_size = rate_values / denominator
    decays = 1.0 - step_size[:, None, :] * keys_sq[:, :, None]
    drives = (step_size * inputs)[:, None, :] * key_blk[:, :, None]
    return keys_sq, denominator, step_size, decays, drives


def reverse_states(decays, emitted, carried):
    following = jnp.concatenate([decays[1:], jnp.ones_like(decays[:1])], axis=0)
    products, accumulated = lax.associative_scan(affine, (following[::-1], emitted[::-1]), axis=0)
    return (accumulated + products * carried[None])[::-1]


def block_grads(inputs, rate_values, key_blk, query_blk, grad_blk, start_state, carried):
    keys_sq, denominator, step_size, decays, drives = block_setup(inputs, rate_values, key_blk)
    products, accumulated = lax.associative_scan(affine, (decays, drives), axis=0)
    states = accumulated + products * start_state[None]
    previous = jnp.concatenate([start_state[None], states[:-1]], axis=0)
    emitted = grad_blk[:, None, :] * query_blk[:, :, None]
    state_grads = reverse_states(decays, emitted, carried)
    key_dot = jnp.sum(state_grads * key_blk[:, :, None], axis=1)
    weighted = state_grads * previous
    weighted_sum = jnp.sum(weighted * keys_sq[:, :, None], axis=1)
    grad_in = step_size * key_dot
    grad_step = inputs * key_dot - weighted_sum
    grad_rate = grad_step / (denominator * denominator)
    term_drive = jnp.sum(state_grads * (step_size * inputs)[:, None, :], axis=2)
    term_decay = jnp.sum(weighted * step_size[:, None, :], axis=2)
    term_norm = jnp.sum(grad_step * step_size * step_size, axis=1)
    grad_key = term_drive - 2.0 * key_blk * (term_decay + term_norm[:, None])
    grad_query = jnp.sum(grad_blk[:, None, :] * states, axis=2)
    return decays[0] * state_grads[0], (grad_in, grad_rate, grad_key, grad_query)


def one_sequence(sequence):
    inputs, step_rate, key_rows, query_rows, grad_out = sequence
    num_blocks = inputs.shape[0] // BLOCK
    channels = inputs.shape[1]
    state_dim = key_rows.shape[1]

    def to_blocks(array_in):
        return array_in.astype(jnp.float32).reshape(num_blocks, BLOCK, array_in.shape[1])

    blocked = (to_blocks(inputs), to_blocks(step_rate), to_blocks(key_rows), to_blocks(query_rows), to_blocks(grad_out))

    def forward(carried, block_in):
        _, _, _, decays, drives = block_setup(block_in[0], block_in[1], block_in[2])
        products, accumulated = lax.associative_scan(affine, (decays, drives), axis=0)
        return accumulated[-1] + products[-1] * carried, carried

    zero_state = jnp.zeros((state_dim, channels), jnp.float32)
    _, block_starts = lax.scan(forward, zero_state, blocked[:3])

    def backward(carried, block_in):
        return block_grads(block_in[0], block_in[1], block_in[2], block_in[3], block_in[4], block_in[5], carried)

    _, results = lax.scan(backward, zero_state, blocked + (block_starts,), reverse=True)
    grad_in, grad_rate, grad_key, grad_query = results
    return (grad_in.reshape(-1, channels).astype(jnp.bfloat16),
            grad_rate.reshape(-1, channels).astype(jnp.bfloat16),
            grad_key.reshape(-1, state_dim),
            grad_query.reshape(-1, state_dim))


def reference(inputs, step_rate, key_rows, query_rows, grad_out):
    return lax.map(one_sequence, (inputs, step_rate, key_rows, query_rows, grad_out))
```

```python
import jax
import jax.numpy as jnp
from jax import lax
from jax.experimental import pallas as pl
from jax.experimental.pallas import tpu as pltpu
from jax.sharding import PartitionSpec as P

MESH = pl.DeviceIdType.MESH
F32 = jnp.float32
BF16 = jnp.bfloat16

SEG = 8
LEN = 16
N = 16
LANES = 128
PAIRS = 4
WIDE = 256
CTX = 16
TOKENS = SEG * LEN


def kernel(
    heads,
    x_ref, rate_ref, k_ref, q_ref, g_ref,
    oi_ref, or_ref, ok_ref, oq_ref,
    kT, k2T, qT, knT,
    x32, g32, r32,
    stepP, uP, gP, xP, invP,
    sumP, sumL, sumB,
    preP, preL, postP, postB,
    send1, recv1, send2, recv2,
    sIn, gIn, kpS,
    accQ, accK, accN,
    outI, outR, sendI, sendR,
    sums, recvS,
    s1_sem, r1_sem, s2_sem, r2_sem,
    hi_send, hi_recv, hr_send, hr_recv, own_sem, rs_send, rs_recv,
):
    me = lax.axis_index("ctx")
    hd = lax.axis_index("head")
    rows_out = TOKENS // heads

    barrier = pltpu.get_barrier_semaphore()
    for d in range(1, CTX):
        pl.semaphore_signal(barrier, inc=1, device_id={"ctx": lax.rem(me + d, CTX)}, device_id_type=MESH)
    for d in range(1, heads):
        pl.semaphore_signal(barrier, inc=1, device_id={"head": lax.rem(hd + d, heads)}, device_id_type=MESH)

    row = lax.broadcasted_iota(jnp.int32, (TOKENS, TOKENS), 0)
    col = lax.broadcasted_iota(jnp.int32, (TOKENS, TOKENS), 1)
    perm = jnp.where(col == (row % SEG) * LEN + row // SEG, 1.0, 0.0).astype(BF16)
    kp = jnp.dot(perm, k_ref[0], preferred_element_type=F32).astype(BF16)
    qp = jnp.dot(perm, q_ref[0], preferred_element_type=F32).astype(BF16)
    state_row = lax.broadcasted_iota(jnp.int32, (N, LANES), 0)
    norm = jnp.zeros((TOKENS, LANES), F32)
    for n in range(N):
        pick = jnp.where(state_row == n, 1.0, 0.0).astype(BF16)
        kn = jnp.dot(kp, pick, preferred_element_type=F32)
        qn = jnp.dot(qp, pick, preferred_element_type=F32)
        k2 = kn * kn
        norm = norm + k2
        for i in range(LEN):
            kT[i * N + n] = kn[i * SEG:(i + 1) * SEG]
            k2T[i * N + n] = k2[i * SEG:(i + 1) * SEG]
            qT[i * N + n] = qn[i * SEG:(i + 1) * SEG]
    for i in range(LEN):
        knT[i] = norm[i * SEG:(i + 1) * SEG]

    def first_pass(it, _):
        p = lax.rem(me // 4 + (PAIRS - 1 - it), PAIRS)
        lane0 = pl.multiple_of(p * WIDE, WIDE)
        for c in range(2):
            lanes = pl.ds(pl.multiple_of(lane0 + c * LANES, LANES), LANES)
            x32[c] = x_ref[0, :, lanes].astype(F32)
            g32[c] = g_ref[0, :, lanes].astype(F32)
            r32[c] = rate_ref[0, :, lanes]
        base = p * (2 * LEN)
        for i in range(LEN):
            for c in range(2):
                at = base + 2 * i + c
                rate = r32[c, pl.ds(i, SEG, stride=LEN), :]
                xv = x32[c, pl.ds(i, SEG, stride=LEN), :]
                gv = g32[c, pl.ds(i, SEG, stride=LEN), :]
                inv = 1.0 / (1.0 + rate * knT[i])
                step = rate * inv
                stepP[at] = step
                invP[at] = inv
                uP[at] = step * xv
                xP[at] = xv
                gP[at] = gv

        def n_group(ng, _):
            n0 = ng * 4
            prod = [None] * 8
            end = [None] * 8
            back = [None] * 8
            for i in range(LEN):
                step = [stepP[base + 2 * i + c] for c in range(2)]
                u = [uP[base + 2 * i + c] for c in range(2)]
                gv = [gP[base + 2 * i + c] for c in range(2)]
                for a in range(4):
                    kk = kT[i * N + n0 + a]
                    k2 = k2T[i * N + n0 + a]
                    qq = qT[i * N + n0 + a]
                    for c in range(2):
                        j = 2 * a + c
                        dec = 1.0 - step[c] * k2
                        emit = gv[c] * qq
                        drive = u[c] * kk
                        if i == 0:
                            prod[j] = dec
                            end[j] = drive
                            back[j] = emit * dec
                        else:
                            prod[j] = prod[j] * dec
                            end[j] = end[j] * dec + drive
                            back[j] = back[j] + emit * prod[j]
            for a in range(4):
                for c in range(2):
                    at = pl.multiple_of((c * N + n0 + a) * SEG, SEG)
                    sumP[pl.ds(at, SEG), :] = prod[2 * a + c]
                    sumL[pl.ds(at, SEG), :] = end[2 * a + c]
                    sumB[pl.ds(at, SEG), :] = back[2 * a + c]
            return 0

        lax.fori_loop(0, N // 4, n_group, 0)

        for j in range(4):
            o = p * 4 + j
            tile = j * 8 * SEG
            run_p = jnp.ones((SEG, LANES), F32)
            run_l = jnp.zeros((SEG, LANES), F32)
            ps, bs = [], []
            for s in range(SEG):
                pv = sumP[pl.ds(tile + s, SEG, stride=SEG), :]
                lv = sumL[pl.ds(tile + s, SEG, stride=SEG), :]
                ps.append(pv)
                bs.append(sumB[pl.ds(tile + s, SEG, stride=SEG), :])
                preP[o * SEG + s] = run_p
                preL[o * SEG + s] = run_l
                run_l = run_l * pv + lv
                run_p = run_p * pv
            send1[o, 0] = run_p
            send1[o, 1] = run_l
            run_p = jnp.ones((SEG, LANES), F32)
            run_b = jnp.zeros((SEG, LANES), F32)
            for s in reversed(range(SEG)):
                postP[o * SEG + s] = run_p
                postB[o * SEG + s] = run_b
                run_b = run_b * ps[s] + bs[s]
                run_p = run_p * ps[s]
            send1[o, 2] = run_b

        @pl.when(it == 0)
        def _():
            pl.semaphore_wait(barrier, CTX - 1 + heads - 1)

        for j in range(4):
            o = p * 4 + j

            @pl.when(o != me)
            def _():
                to_owner(o).start()

            @pl.when(o == me)
            def _():
                recv1[o] = send1[o]
        return 0

    def to_owner(o):
        return pltpu.make_async_remote_copy(
            src_ref=send1.at[o], dst_ref=recv1.at[me], send_sem=s1_sem.at[o], recv_sem=r1_sem.at[me],
            device_id={"ctx": o}, device_id_type=MESH)

    def from_group(o):
        return pltpu.make_async_remote_copy(
            src_ref=send1.at[o], dst_ref=recv1.at[o], send_sem=s1_sem.at[o], recv_sem=r1_sem.at[o],
            device_id={"ctx": o}, device_id_type=MESH)

    def to_group(o):
        return pltpu.make_async_remote_copy(
            src_ref=send2.at[o], dst_ref=recv2.at[me], send_sem=s2_sem.at[o], recv_sem=r2_sem.at[me],
            device_id={"ctx": o}, device_id_type=MESH)

    def from_owner(o):
        return pltpu.make_async_remote_copy(
            src_ref=send2.at[o], dst_ref=recv2.at[o], send_sem=s2_sem.at[o], recv_sem=r2_sem.at[o],
            device_id={"ctx": o}, device_id_type=MESH)

    lax.fori_loop(0, PAIRS, first_pass, 0)

    zero = jnp.zeros((SEG, LANES), F32)

    def clear(i, _):
        for n in range(N):
            accQ[i * N + n] = zero
            accK[i * N + n] = zero
        accN[i] = zero
        return 0

    lax.fori_loop(0, LEN, clear, 0)

    for d in range(1, CTX):
        from_group(lax.rem(me + d, CTX)).wait_recv()
    state = zero
    grad = zero
    for c in range(CTX):
        send2[c, 0] = state
        state = state * recv1[c, 0] + recv1[c, 1]
    for c in reversed(range(CTX)):
        send2[c, 1] = grad
        grad = grad * recv1[c, 0] + recv1[c, 2]
    for d in range(1, CTX):
        to_group(lax.rem(me + d, CTX)).start()
    recv2[me] = send2[me]

    def head_copy(array, p, h, src_buf, dst, ssem, rsem):
        return pltpu.make_async_remote_copy(
            src_ref=src_buf.at[p, pl.ds(pl.multiple_of(h * rows_out, rows_out), rows_out), :],
            dst_ref=dst.at[0, :, pl.ds(pl.multiple_of(array * (PAIRS * WIDE) + p * WIDE, WIDE), WIDE)],
            send_sem=ssem.at[p, h], recv_sem=rsem.at[p, array],
            device_id={"head": h}, device_id_type=MESH)

    def own_copy(p, which, src_buf, dst):
        return pltpu.make_async_copy(
            src_buf.at[p, pl.ds(pl.multiple_of(hd * rows_out, rows_out), rows_out), :],
            dst.at[0, :, pl.ds(pl.multiple_of(hd * (PAIRS * WIDE) + p * WIDE, WIDE), WIDE)],
            own_sem.at[p, which])

    def second_pass(it, _):
        p = lax.rem(me // 4 + it, PAIRS)
        base = p * (2 * LEN)
        for j in range(4):
            o = p * 4 + j

            @pl.when(o != me)
            def _():
                from_owner(o).wait_recv()

            s0 = recv2[o, 0]
            g0 = recv2[o, 1]
            tile = j * 8 * SEG
            for s in range(SEG):
                at = o * SEG + s
                sIn[pl.ds(tile + s, SEG, stride=SEG), :] = preP[at] * s0 + preL[at]
                gIn[pl.ds(tile + s, SEG, stride=SEG), :] = postP[at] * g0 + postB[at]

        def forward(i, states):
            states = list(states)
            step = [stepP[base + 2 * i + c] for c in range(2)]
            u = [uP[base + 2 * i + c] for c in range(2)]
            gv = [gP[base + 2 * i + c] for c in range(2)]
            for n in range(N):
                kk = kT[i * N + n]
                total = accQ[i * N + n]
                for c in range(2):
                    j = n * 2 + c
                    kprev = kk * states[j]
                    kpS[i * (2 * N) + j] = kprev
                    new = states[j] + kk * (u[c] - step[c] * kprev)
                    states[j] = new
                    total = total + gv[c] * new
                accQ[i * N + n] = total
            return tuple(states)

        start = tuple(sIn[pl.ds((c * N + n) * SEG, SEG), :] for n in range(N) for c in range(2))
        lax.fori_loop(0, LEN, forward, start)

        def backward(it2, grads):
            i = LEN - 1 - it2
            grads = list(grads)
            step = [stepP[base + 2 * i + c] for c in range(2)]
            twice = [s + s for s in step]
            u = [uP[base + 2 * i + c] for c in range(2)]
            gv = [gP[base + 2 * i + c] for c in range(2)]
            key_dot = [None, None]
            weighted = [None, None]
            for n in range(N):
                kk = kT[i * N + n]
                qq = qT[i * N + n]
                total = accK[i * N + n]
                for c in range(2):
                    j = n * 2 + c
                    kprev = kpS[i * (2 * N) + j]
                    grad = grads[j] + gv[c] * qq
                    gk = grad * kk
                    wk = gk * kprev
                    key_dot[c] = gk if n == 0 else key_dot[c] + gk
                    weighted[c] = wk if n == 0 else weighted[c] + wk
                    total = total + grad * (u[c] - twice[c] * kprev)
                    grads[j] = grad - kk * (step[c] * gk)
                accK[i * N + n] = total
            norm_sum = accN[i]
            for c in range(2):
                at = base + 2 * i + c
                inv = invP[at]
                outI[c, pl.ds(i, SEG, stride=LEN), :] = step[c] * key_dot[c]
                grad_step = xP[at] * key_dot[c] - weighted[c]
                outR[c, pl.ds(i, SEG, stride=LEN), :] = grad_step * (inv * inv)
                norm_sum = norm_sum + grad_step * (step[c] * step[c])
            accN[i] = norm_sum
            return tuple(grads)

        start = tuple(gIn[pl.ds((c * N + n) * SEG, SEG), :] for n in range(N) for c in range(2))
        lax.fori_loop(0, LEN, backward, start)
        for c in range(2):
            lanes = pl.ds(c * LANES, LANES)
            sendI[p, :, lanes] = outI[c].astype(BF16)
            sendR[p, :, lanes] = outR[c].astype(BF16)
        for d in range(1, heads):
            h = lax.rem(hd + d, heads)
            pltpu.make_async_remote_copy(
                src_ref=sendI.at[p, pl.ds(pl.multiple_of(h * rows_out, rows_out), rows_out), :],
                dst_ref=oi_ref.at[0, :, pl.ds(pl.multiple_of(hd * (PAIRS * WIDE) + p * WIDE, WIDE), WIDE)],
                send_sem=hi_send.at[p, h], recv_sem=hi_recv.at[p, hd],
                device_id={"head": h}, device_id_type=MESH).start()
            pltpu.make_async_remote_copy(
                src_ref=sendR.at[p, pl.ds(pl.multiple_of(h * rows_out, rows_out), rows_out), :],
                dst_ref=or_ref.at[0, :, pl.ds(pl.multiple_of(hd * (PAIRS * WIDE) + p * WIDE, WIDE), WIDE)],
                send_sem=hr_send.at[p, h], recv_sem=hr_recv.at[p, hd],
                device_id={"head": h}, device_id_type=MESH).start()
        own_copy(p, 0, sendI, oi_ref).start()
        own_copy(p, 1, sendR, or_ref).start()
        return 0

    lax.fori_loop(0, PAIRS, second_pass, 0)

    lane = lax.broadcasted_iota(jnp.int32, (SEG, LANES), 1)

    def reduce_lanes(i, _):
        merged = zero
        norm2 = accN[i] + accN[i]
        for n in range(N):
            key = accK[i * N + n] - kT[i * N + n] * norm2
            merged = jnp.where(lane == n, jnp.sum(key, axis=1, keepdims=True), merged)
            merged = jnp.where(lane == N + n, jnp.sum(accQ[i * N + n], axis=1, keepdims=True), merged)
        sums[pl.ds(i, SEG, stride=LEN), :] = merged
        return 0

    lax.fori_loop(0, LEN, reduce_lanes, 0)

    def sum_copy(h, src):
        return pltpu.make_async_remote_copy(
            src_ref=sums.at[pl.ds(pl.multiple_of(h * rows_out, rows_out), rows_out), :],
            dst_ref=recvS.at[src], send_sem=rs_send.at[h], recv_sem=rs_recv.at[src],
            device_id={"head": h}, device_id_type=MESH)

    for d in range(1, heads):
        sum_copy(lax.rem(hd + d, heads), hd).start()
    recvS[hd] = sums[pl.ds(pl.multiple_of(hd * rows_out, rows_out), rows_out), :]

    for d in range(1, CTX):
        o = lax.rem(me + d, CTX)
        to_owner(o).wait_send()
        to_group(o).wait_send()
    for p in range(PAIRS):
        own_copy(p, 0, sendI, oi_ref).wait()
        own_copy(p, 1, sendR, or_ref).wait()
        for d in range(1, heads):
            h = lax.rem(hd + d, heads)
            for buf, dst, ssem, rsem in ((sendI, oi_ref, hi_send, hi_recv), (sendR, or_ref, hr_send, hr_recv)):
                copy = head_copy(h, p, h, buf, dst, ssem, rsem)
                copy.wait_send()
                copy.wait_recv()
    for d in range(1, heads):
        h = lax.rem(hd + d, heads)
        copy = sum_copy(h, h)
        copy.wait_send()
        copy.wait_recv()
    total = recvS[0]
    for h in range(1, heads):
        total = total + recvS[h]
    ok_ref[0] = total[:, :N]
    oq_ref[0] = total[:, N:2 * N]


def shards(heads):
    def run(inputs, step_rate, key_rows, query_rows, grad_out):
        rows_out = TOKENS // heads
        width = heads * PAIRS * WIDE
        vmem = pl.BlockSpec(memory_space=pltpu.VMEM)
        hbm = pl.BlockSpec(memory_space=pl.ANY)
        tile = (SEG, LANES)

        def regs(*lead):
            return pltpu.VMEM(lead + tile, F32)

        dma = pltpu.SemaphoreType.DMA
        return pl.pallas_call(
            lambda *refs: kernel(heads, *refs),
            out_shape=(
                jax.ShapeDtypeStruct((1, rows_out, width), BF16),
                jax.ShapeDtypeStruct((1, rows_out, width), BF16),
                jax.ShapeDtypeStruct((1, rows_out, N), F32),
                jax.ShapeDtypeStruct((1, rows_out, N), F32),
            ),
            in_specs=[vmem] * 5,
            out_specs=(hbm, hbm, vmem, vmem),
            scratch_shapes=[
                regs(LEN * N), regs(LEN * N), regs(LEN * N), regs(LEN),
                *[pltpu.VMEM((2, TOKENS, LANES), F32) for _ in range(3)],
                *[regs(PAIRS * 2 * LEN) for _ in range(5)],
                *[pltpu.VMEM((2 * N * SEG, LANES), F32) for _ in range(3)],
                *[regs(CTX * SEG) for _ in range(4)],
                regs(CTX, 3), regs(CTX, 3), regs(CTX, 2), regs(CTX, 2),
                pltpu.VMEM((2 * N * SEG, LANES), F32), pltpu.VMEM((2 * N * SEG, LANES), F32),
                regs(LEN * 2 * N),
                regs(LEN * N), regs(LEN * N), regs(LEN),
                pltpu.VMEM((2, TOKENS, LANES), F32), pltpu.VMEM((2, TOKENS, LANES), F32),
                pltpu.VMEM((PAIRS, TOKENS, WIDE), BF16), pltpu.VMEM((PAIRS, TOKENS, WIDE), BF16),
                pltpu.VMEM((TOKENS, LANES), F32), pltpu.VMEM((heads, rows_out, LANES), F32),
                dma((CTX,)), dma((CTX,)), dma((CTX,)), dma((CTX,)),
                dma((PAIRS, heads)), dma((PAIRS, heads)), dma((PAIRS, heads)), dma((PAIRS, heads)),
                dma((PAIRS, 2)), dma((heads,)), dma((heads,)),
            ],
            compiler_params=pltpu.CompilerParams(
                collective_id=0, has_side_effects=True, vmem_limit_bytes=48 * 1024 * 1024),
        )(inputs, step_rate, key_rows, query_rows, grad_out)

    return run


def solution(mesh):
    placed = (
        P("dp", "ctx", "head"),
        P("dp", "ctx", "head"),
        P("dp", "ctx", None),
        P("dp", "ctx", None),
        P("dp", "ctx", "head"),
    )
    out = P("dp", ("ctx", "head"), None)
    return jax.shard_map(
        shards(mesh.shape["head"]),
        mesh=mesh,
        in_specs=placed,
        out_specs=(out, out, out, out),
        check_vma=False,
    )
```

```python
import jax
import jax.numpy as jnp
from jax import lax
from jax.experimental import pallas as pl
from jax.experimental.pallas import tpu as pltpu
from jax.sharding import PartitionSpec as P

MESH = pl.DeviceIdType.MESH
F32 = jnp.float32
BF16 = jnp.bfloat16

SEG = 8
LEN = 16
N = 16
LANES = 128
PAIRS = 4
WIDE = 256
CTX = 16
STEPS = 2
TOKENS = SEG * LEN


def owner_of(p, j):
    return 2 * (2 * j + p % 2) + p // 2


def kernel(
    heads,
    x_ref, rate_ref, k_ref, q_ref, g_ref,
    oi_ref, or_ref, rs_ref,
    xV, rV, gV, kV, qV,
    kT, k2T, qT, knT, kL,
    x32, g32, r32,
    stepP, uP, gP, xP, invP, decS,
    sumP, sumL, sumB,
    preP, preL, postP, postB,
    send1, recv1, send2, recv2,
    sIn, gIn, kpS,
    accQ, accK, accN,
    outI, outR, sendI, sendR,
    sums,
    in_sem, s1_sem, r1_sem, s2_sem, r2_sem,
    hi_send, hi_recv, hr_send, hr_recv, own_sem, rs_send, rs_recv,
):
    me = lax.axis_index("ctx")
    hd = lax.axis_index("head")
    rows_out = TOKENS // heads
    my_pair = 2 * lax.rem(me, 2) + lax.rem(me // 2, 2)
    my_tile = my_pair * 4 + me // 4

    k_copy = pltpu.make_async_copy(k_ref.at[0], kV, in_sem.at[3 * PAIRS])
    q_copy = pltpu.make_async_copy(q_ref.at[0], qV, in_sem.at[3 * PAIRS + 1])
    k_copy.start()
    q_copy.start()

    def in_copy(p, which):
        ref, buf = ((x_ref, xV), (rate_ref, rV), (g_ref, gV))[which]
        lanes = pl.ds(p * WIDE, WIDE) if isinstance(p, int) else pl.ds(pl.multiple_of(p * WIDE, WIDE), WIDE)
        return pltpu.make_async_copy(ref.at[0, :, lanes], buf.at[p], in_sem.at[p * 3 + which])

    for p in range(PAIRS):
        for which in range(3):
            in_copy(p, which).start()

    barrier = pltpu.get_barrier_semaphore()
    for d in range(1, CTX):
        pl.semaphore_signal(barrier, inc=1, device_id={"ctx": lax.rem(me + d, CTX)}, device_id_type=MESH)
    for d in range(1, heads):
        pl.semaphore_signal(barrier, inc=1, device_id={"head": lax.rem(hd + d, heads)}, device_id_type=MESH)

    row = lax.broadcasted_iota(jnp.int32, (TOKENS, TOKENS), 0)
    col = lax.broadcasted_iota(jnp.int32, (TOKENS, TOKENS), 1)
    perm = jnp.where(col == (row % SEG) * LEN + row // SEG, 1.0, 0.0).astype(BF16)
    state_row = lax.broadcasted_iota(jnp.int32, (N, LANES), 0)
    state_col = lax.broadcasted_iota(jnp.int32, (N, LANES), 1)
    k_copy.wait()
    q_copy.wait()
    last = (((1,), (1,)), ((), ()))
    kp = lax.dot_general(perm, kV[...], last, preferred_element_type=F32).astype(BF16)
    qp = lax.dot_general(perm, qV[...], last, preferred_element_type=F32).astype(BF16)
    kL[...] = jnp.dot(kp, jnp.where(state_row == state_col, 1.0, 0.0).astype(BF16), preferred_element_type=F32)
    norm = jnp.zeros((TOKENS, LANES), F32)
    for n in range(N):
        pick = jnp.where(state_row == n, 1.0, 0.0).astype(BF16)
        kn = jnp.dot(kp, pick, preferred_element_type=F32)
        qn = jnp.dot(qp, pick, preferred_element_type=F32)
        k2 = kn * kn
        norm = norm + k2
        for i in range(LEN):
            kT[i * N + n] = kn[i * SEG:(i + 1) * SEG]
            k2T[i * N + n] = k2[i * SEG:(i + 1) * SEG]
            qT[i * N + n] = qn[i * SEG:(i + 1) * SEG]
    for i in range(LEN):
        knT[i] = norm[i * SEG:(i + 1) * SEG]

    def to_owner(p, j):
        o = owner_of(p, j)
        return pltpu.make_async_remote_copy(
            src_ref=send1.at[p * 4 + j], dst_ref=recv1.at[me], send_sem=s1_sem.at[p * 4 + j],
            recv_sem=r1_sem.at[me], device_id={"ctx": o}, device_id_type=MESH)

    def from_group(o):
        return pltpu.make_async_remote_copy(
            src_ref=send1.at[0], dst_ref=recv1.at[o], send_sem=s1_sem.at[0], recv_sem=r1_sem.at[o],
            device_id={"ctx": o}, device_id_type=MESH)

    def to_group(o):
        return pltpu.make_async_remote_copy(
            src_ref=send2.at[o], dst_ref=recv2.at[my_tile], send_sem=s2_sem.at[o], recv_sem=r2_sem.at[my_tile],
            device_id={"ctx": o}, device_id_type=MESH)

    def from_owner(p, j):
        return pltpu.make_async_remote_copy(
            src_ref=send2.at[0], dst_ref=recv2.at[p * 4 + j], send_sem=s2_sem.at[0],
            recv_sem=r2_sem.at[p * 4 + j], device_id={"ctx": owner_of(p, j)}, device_id_type=MESH)

    def own_scan():
        for d in range(1, CTX):
            from_group(lax.rem(me + d, CTX)).wait_recv()
        state = jnp.zeros((SEG, LANES), F32)
        grad = state
        for c in range(CTX):
            send2[c, 0] = state
            state = state * recv1[c, 0] + recv1[c, 1]
        for c in reversed(range(CTX)):
            send2[c, 1] = grad
            grad = grad * recv1[c, 0] + recv1[c, 2]
        for d in range(1, CTX):
            to_group(lax.rem(me + d, CTX)).start()
        recv2[my_tile] = send2[me]

    def first_pass(p, _):
        for which in range(3):
            in_copy(p, which).wait()
        for c in range(2):
            lanes = pl.ds(c * LANES, LANES)
            x32[c] = xV[p, :, lanes].astype(F32)
            g32[c] = gV[p, :, lanes].astype(F32)
            r32[c] = rV[p, :, lanes]
        base = p * (2 * LEN)
        for i in range(LEN):
            for c in range(2):
                at = base + 2 * i + c
                rate = r32[c, pl.ds(i, SEG, stride=LEN), :]
                xv = x32[c, pl.ds(i, SEG, stride=LEN), :]
                gv = g32[c, pl.ds(i, SEG, stride=LEN), :]
                inv = 1.0 / (1.0 + rate * knT[i])
                step = rate * inv
                stepP[at] = step
                invP[at] = inv
                uP[at] = step * xv
                xP[at] = xv
                gP[at] = gv

        def n_group(ng, _):
            n0 = ng * 4
            prod = [None] * 8
            end = [None] * 8
            back = [None] * 8
            for i in range(LEN):
                step = [stepP[base + 2 * i + c] for c in range(2)]
                u = [uP[base + 2 * i + c] for c in range(2)]
                gv = [gP[base + 2 * i + c] for c in range(2)]
                for a in range(4):
                    kk = kT[i * N + n0 + a]
                    k2 = k2T[i * N + n0 + a]
                    qq = qT[i * N + n0 + a]
                    for c in range(2):
                        j = 2 * a + c
                        dec = 1.0 - step[c] * k2
                        decS[(p * LEN + i) * (2 * N) + 2 * n0 + j] = dec
                        emit = gv[c] * qq
                        drive = u[c] * kk
                        if i == 0:
                            prod[j] = dec
                            end[j] = drive
                            back[j] = emit * dec
                        else:
                            prod[j] = prod[j] * dec
                            end[j] = end[j] * dec + drive
                            back[j] = back[j] + emit * prod[j]
            for a in range(4):
                for c in range(2):
                    at = pl.multiple_of((c * N + n0 + a) * SEG, SEG)
                    sumP[pl.ds(at, SEG), :] = prod[2 * a + c]
                    sumL[pl.ds(at, SEG), :] = end[2 * a + c]
                    sumB[pl.ds(at, SEG), :] = back[2 * a + c]
            return 0

        lax.fori_loop(0, N // 4, n_group, 0)

        for j in range(4):
            o = p * 4 + j
            tile = j * 8 * SEG
            run_p = jnp.ones((SEG, LANES), F32)
            run_l = jnp.zeros((SEG, LANES), F32)
            ps, bs = [], []
            for s in range(SEG):
                pv = sumP[pl.ds(tile + s, SEG, stride=SEG), :]
                lv = sumL[pl.ds(tile + s, SEG, stride=SEG), :]
                ps.append(pv)
                bs.append(sumB[pl.ds(tile + s, SEG, stride=SEG), :])
                preP[o * SEG + s] = run_p
                preL[o * SEG + s] = run_l
                run_l = run_l * pv + lv
                run_p = run_p * pv
            send1[o, 0] = run_p
            send1[o, 1] = run_l
            run_p = jnp.ones((SEG, LANES), F32)
            run_b = jnp.zeros((SEG, LANES), F32)
            for s in reversed(range(SEG)):
                postP[o * SEG + s] = run_p
                postB[o * SEG + s] = run_b
                run_b = run_b * ps[s] + bs[s]
                run_p = run_p * ps[s]
            send1[o, 2] = run_b

        @pl.when(p == 0)
        def _():
            pl.semaphore_wait(barrier, CTX - 1 + heads - 1)

        for j in range(4):
            @pl.when(owner_of(p, j) != me)
            def _():
                to_owner(p, j).start()

            @pl.when(owner_of(p, j) == me)
            def _():
                recv1[me] = send1[p * 4 + j]

        @pl.when((p >= 2) & (my_pair == p - 2))
        def _():
            own_scan()
        return 0

    lax.fori_loop(0, PAIRS, first_pass, 0)

    zero = jnp.zeros((SEG, LANES), F32)

    def clear(i, _):
        for n in range(N):
            accQ[i * N + n] = zero
            accK[i * N + n] = zero
        accN[i] = zero
        return 0

    lax.fori_loop(0, LEN, clear, 0)

    @pl.when(my_pair == 2)
    def _():
        own_scan()

    def head_copy(p, h, owner, src_buf, dst, ssem, rsem):
        return pltpu.make_async_remote_copy(
            src_ref=src_buf.at[p, pl.ds(pl.multiple_of(h * rows_out, rows_out), rows_out), :],
            dst_ref=dst.at[0, :, pl.ds(pl.multiple_of(owner * (PAIRS * WIDE) + p * WIDE, WIDE), WIDE)],
            send_sem=ssem.at[p, h], recv_sem=rsem.at[p, owner],
            device_id={"head": h}, device_id_type=MESH)

    def own_copy(p, which, src_buf, dst):
        return pltpu.make_async_copy(
            src_buf.at[p, pl.ds(pl.multiple_of(hd * rows_out, rows_out), rows_out), :],
            dst.at[0, :, pl.ds(pl.multiple_of(hd * (PAIRS * WIDE) + p * WIDE, WIDE), WIDE)],
            own_sem.at[p, which])

    arrays = ((sendI, oi_ref, hi_send, hi_recv), (sendR, or_ref, hr_send, hr_recv))

    def second_pass(p, _):
        base = p * (2 * LEN)
        for j in range(4):
            o = p * 4 + j

            @pl.when(owner_of(p, j) != me)
            def _():
                from_owner(p, j).wait_recv()

            s0 = recv2[o, 0]
            g0 = recv2[o, 1]
            tile = j * 8 * SEG
            for s in range(SEG):
                at = o * SEG + s
                sIn[pl.ds(tile + s, SEG, stride=SEG), :] = preP[at] * s0 + preL[at]
                gIn[pl.ds(tile + s, SEG, stride=SEG), :] = postP[at] * g0 + postB[at]

        def forward(i, states):
            states = list(states)
            u = [uP[base + 2 * i + c] for c in range(2)]
            gv = [gP[base + 2 * i + c] for c in range(2)]
            for n in range(N):
                kk = kT[i * N + n]
                total = accQ[i * N + n]
                for c in range(2):
                    j = n * 2 + c
                    kpS[i * (2 * N) + j] = kk * states[j]
                    states[j] = decS[(p * LEN + i) * (2 * N) + j] * states[j] + u[c] * kk
                    total = total + gv[c] * states[j]
                accQ[i * N + n] = total
            return tuple(states)

        start = tuple(sIn[pl.ds((c * N + n) * SEG, SEG), :] for n in range(N) for c in range(2))
        def forward_some(b, states):
            for r in range(STEPS):
                states = forward(b * STEPS + r, states)
            return states

        lax.fori_loop(0, LEN // STEPS, forward_some, start)

        def backward(it2, grads):
            i = LEN - 1 - it2
            grads = list(grads)
            step = [stepP[base + 2 * i + c] for c in range(2)]
            twice = [s + s for s in step]
            u = [uP[base + 2 * i + c] for c in range(2)]
            gv = [gP[base + 2 * i + c] for c in range(2)]
            key_dot = [None, None]
            weighted = [None, None]
            for n in range(N):
                kk = kT[i * N + n]
                qq = qT[i * N + n]
                total = accK[i * N + n]
                for c in range(2):
                    j = n * 2 + c
                    kprev = kpS[i * (2 * N) + j]
                    grad = grads[j] + gv[c] * qq
                    gk = grad * kk
                    wk = gk * kprev
                    key_dot[c] = gk if n == 0 else key_dot[c] + gk
                    weighted[c] = wk if n == 0 else weighted[c] + wk
                    total = total + grad * (u[c] - twice[c] * kprev)
                    grads[j] = grad * decS[(p * LEN + i) * (2 * N) + j]
                accK[i * N + n] = total
            norm_sum = accN[i]
            for c in range(2):
                at = base + 2 * i + c
                inv = invP[at]
                outI[c, pl.ds(i, SEG, stride=LEN), :] = step[c] * key_dot[c]
                grad_step = xP[at] * key_dot[c] - weighted[c]
                outR[c, pl.ds(i, SEG, stride=LEN), :] = grad_step * (inv * inv)
                norm_sum = norm_sum + grad_step * (step[c] * step[c])
            accN[i] = norm_sum
            return tuple(grads)

        start = tuple(gIn[pl.ds((c * N + n) * SEG, SEG), :] for n in range(N) for c in range(2))
        def backward_some(b, grads):
            for r in range(STEPS):
                grads = backward(b * STEPS + r, grads)
            return grads

        lax.fori_loop(0, LEN // STEPS, backward_some, start)
        for c in range(2):
            lanes = pl.ds(c * LANES, LANES)
            sendI[p, :, lanes] = outI[c].astype(BF16)
            sendR[p, :, lanes] = outR[c].astype(BF16)
        for d in range(1, heads):
            for src_buf, dst, ssem, rsem in arrays:
                head_copy(p, lax.rem(hd + d, heads), hd, src_buf, dst, ssem, rsem).start()
        own_copy(p, 0, sendI, oi_ref).start()
        own_copy(p, 1, sendR, or_ref).start()

        @pl.when((p == 0) & (my_pair == 3))
        def _():
            own_scan()
        return 0

    lax.fori_loop(0, PAIRS, second_pass, 0)

    ones = jnp.ones((2 * LANES, LANES), BF16)
    lane = lax.broadcasted_iota(jnp.int32, (TOKENS, LANES), 1)

    def lane_sums(parts):
        whole = jnp.concatenate(parts, axis=0)
        high = whole.astype(BF16)
        low = (whole - high.astype(F32)).astype(BF16)
        return jnp.dot(jnp.concatenate([high, low], axis=1), ones, preferred_element_type=F32)

    merged = lane_sums([accN[i] for i in range(LEN)]) * (-2.0 * kL[...])
    for n in range(N):
        merged = jnp.where(lane == n, merged + lane_sums([accK[i * N + n] for i in range(LEN)]), merged)
        merged = jnp.where(lane == N + n, lane_sums([accQ[i * N + n] for i in range(LEN)]), merged)
    for i in range(LEN):
        sums[pl.ds(i, SEG, stride=LEN), :] = merged[i * SEG:(i + 1) * SEG]

    def sum_copy(h, src):
        return pltpu.make_async_remote_copy(
            src_ref=sums.at[pl.ds(pl.multiple_of(h * rows_out, rows_out), rows_out), :], dst_ref=rs_ref.at[src], send_sem=rs_send.at[h], recv_sem=rs_recv.at[src],
            device_id={"head": h}, device_id_type=MESH)

    for d in range(1, heads):
        sum_copy(lax.rem(hd + d, heads), hd).start()
    rs_ref[hd] = sums[pl.ds(pl.multiple_of(hd * rows_out, rows_out), rows_out), :]

    for p in range(PAIRS):
        for j in range(4):
            @pl.when(owner_of(p, j) != me)
            def _():
                to_owner(p, j).wait_send()
    for d in range(1, CTX):
        to_group(lax.rem(me + d, CTX)).wait_send()
    for p in range(PAIRS):
        own_copy(p, 0, sendI, oi_ref).wait()
        own_copy(p, 1, sendR, or_ref).wait()
        for d in range(1, heads):
            h = lax.rem(hd + d, heads)
            for src_buf, dst, ssem, rsem in arrays:
                copy = head_copy(p, h, h, src_buf, dst, ssem, rsem)
                copy.wait_send()
                copy.wait_recv()
    for d in range(1, heads):
        h = lax.rem(hd + d, heads)
        copy = sum_copy(h, h)
        copy.wait_send()
        copy.wait_recv()


def finish(heads, i_ref, r_ref, s_ref, oi_ref, or_ref, ok_ref, oq_ref, small, sem):
    first = pltpu.make_async_copy(i_ref, oi_ref, sem.at[0])
    second = pltpu.make_async_copy(r_ref, or_ref, sem.at[1])
    first.start()
    second.start()
    total = s_ref[0]
    for h in range(1, heads):
        total = total + s_ref[h]
    turned = total.T
    small[0] = turned[:N]
    small[1] = turned[N:2 * N]
    third = pltpu.make_async_copy(small.at[0], ok_ref.at[0], sem.at[2])
    fourth = pltpu.make_async_copy(small.at[1], oq_ref.at[0], sem.at[3])
    third.start()
    fourth.start()
    for copy in (first, second, third, fourth):
        copy.wait()


def shards(heads):
    def run(inputs, step_rate, key_rows, query_rows, grad_out):
        rows_out = TOKENS // heads
        width = heads * PAIRS * WIDE
        vmem = pl.BlockSpec(memory_space=pltpu.VMEM)
        hbm = pl.BlockSpec(memory_space=pltpu.HBM)
        tile = (SEG, LANES)

        def regs(*lead):
            return pltpu.VMEM(lead + tile, F32)

        dma = pltpu.SemaphoreType.DMA
        wide = jax.ShapeDtypeStruct((1, rows_out, width), BF16)
        small = jax.ShapeDtypeStruct((1, N, rows_out), F32)
        grads_in, grads_rate, partial = pl.pallas_call(
            lambda *refs: kernel(heads, *refs),
            out_shape=(
                pltpu.VMEM((1, rows_out, width), BF16),
                pltpu.VMEM((1, rows_out, width), BF16),
                pltpu.VMEM((heads, rows_out, LANES), F32),
            ),
            in_specs=[hbm] * 5,
            out_specs=(vmem, vmem, vmem),
            scratch_shapes=[
                pltpu.VMEM((PAIRS, TOKENS, WIDE), BF16), pltpu.VMEM((PAIRS, TOKENS, WIDE), F32),
                pltpu.VMEM((PAIRS, TOKENS, WIDE), BF16),
                pltpu.VMEM((N, TOKENS), BF16), pltpu.VMEM((N, TOKENS), BF16),
                regs(LEN * N), regs(LEN * N), regs(LEN * N), regs(LEN), pltpu.VMEM((TOKENS, LANES), F32),
                *[pltpu.VMEM((2, TOKENS, LANES), F32) for _ in range(3)],
                *[regs(PAIRS * 2 * LEN) for _ in range(5)],
                regs(PAIRS * LEN * 2 * N),
                *[pltpu.VMEM((2 * N * SEG, LANES), F32) for _ in range(3)],
                *[regs(CTX * SEG) for _ in range(4)],
                regs(CTX, 3), regs(CTX, 3), regs(CTX, 2), regs(CTX, 2),
                pltpu.VMEM((2 * N * SEG, LANES), F32), pltpu.VMEM((2 * N * SEG, LANES), F32),
                regs(LEN * 2 * N),
                regs(LEN * N), regs(LEN * N), regs(LEN),
                pltpu.VMEM((2, TOKENS, LANES), F32), pltpu.VMEM((2, TOKENS, LANES), F32),
                pltpu.VMEM((PAIRS, TOKENS, WIDE), BF16), pltpu.VMEM((PAIRS, TOKENS, WIDE), BF16),
                pltpu.VMEM((TOKENS, LANES), F32),
                dma((3 * PAIRS + 2,)),
                dma((CTX,)), dma((CTX,)), dma((CTX,)), dma((CTX,)),
                dma((PAIRS, heads)), dma((PAIRS, heads)), dma((PAIRS, heads)), dma((PAIRS, heads)),
                dma((PAIRS, 2)), dma((heads,)), dma((heads,)),
            ],
            compiler_params=pltpu.CompilerParams(
                collective_id=0, has_side_effects=True, vmem_limit_bytes=48 * 1024 * 1024),
        )(*(
            pltpu.with_memory_space_constraint(a, pltpu.HBM)
            for a in (inputs, step_rate, jnp.swapaxes(key_rows, 1, 2), jnp.swapaxes(query_rows, 1, 2), grad_out)
        ))
        grads_in, grads_rate, keys, queries = pl.pallas_call(
            lambda *refs: finish(heads, *refs),
            out_shape=(wide, wide, small, small),
            in_specs=[vmem, vmem, vmem],
            out_specs=(hbm, hbm, hbm, hbm),
            scratch_shapes=[pltpu.VMEM((2, N, rows_out), F32), dma((4,))],
        )(*(pltpu.with_memory_space_constraint(a, pltpu.VMEM) for a in (grads_in, grads_rate, partial)))
        return grads_in, grads_rate, jnp.swapaxes(keys, 1, 2), jnp.swapaxes(queries, 1, 2)

    return run


def solution(mesh):
    placed = (
        P("dp", "ctx", "head"),
        P("dp", "ctx", "head"),
        P("dp", "ctx", None),
        P("dp", "ctx", None),
        P("dp", "ctx", "head"),
    )
    out = P("dp", ("ctx", "head"), None)
    return jax.shard_map(
        shards(mesh.shape["head"]),
        mesh=mesh,
        in_specs=placed,
        out_specs=(out, out, out, out),
        check_vma=False,
    )
```

```python
import jax
import jax.numpy as jnp
from jax import lax
from jax.experimental import pallas as pl
from jax.experimental.pallas import tpu as pltpu
from jax.sharding import PartitionSpec as P

MESH = pl.DeviceIdType.MESH
F32 = jnp.float32
BF16 = jnp.bfloat16

SEG = 8
LEN = 16
N = 16
LANES = 128
PAIRS = 4
WIDE = 256
CTX = 16
CHIPS = CTX // 2
STEPS = 4
TOKENS = SEG * LEN


def kernel(
    heads,
    x_ref, rate_ref, k_ref, q_ref, g_ref,
    oi_ref, or_ref, rs_ref,
    xV, rV, gV, kV, qV,
    kT, k2T, qT, knT, kL,
    x32, g32, r32,
    stepP, uP, gP, xP, invP, decS,
    sumP, sumL, sumB,
    preP, preL, postP, postB,
    send1, recvC, send2, recv2, send3, recv3, sendS, entry,
    sIn, gIn, kpS,
    accQ, accK, accN,
    outI, outR, sendI, sendR,
    sums,
    in_sem, c1_send, c1_recv, s2_sem, r2_sem, s3_sem, r3_sem, c4_send, c4_recv,
    hi_send, hi_recv, hr_send, hr_recv, own_sem, rs_send, rs_recv,
):
    me = lax.axis_index("ctx")
    hd = lax.axis_index("head")
    rows_out = TOKENS // heads
    chip = me // 2
    core = lax.rem(me, 2)
    sibling = me + 1 - 2 * core
    near = chip // 4

    def on_chip(d):
        return 2 * lax.rem(chip + d, CHIPS) + core

    barrier = pltpu.get_barrier_semaphore()
    for d in sorted(range(1, CHIPS), key=lambda d: -min(d, CHIPS - d)):
        pl.semaphore_signal(barrier, inc=1, device_id={"ctx": on_chip(d)}, device_id_type=MESH)
    for d in range(1, heads):
        pl.semaphore_signal(barrier, inc=1, device_id={"head": lax.rem(hd + d, heads)}, device_id_type=MESH)
    pl.semaphore_signal(barrier, inc=1, device_id={"ctx": sibling}, device_id_type=MESH)

    def first_order(it):
        return 2 * lax.rem(core + 1 + it // 2, 2) + lax.rem(near + 1 + it, 2)

    k_copy = pltpu.make_async_copy(k_ref.at[0], kV, in_sem.at[3 * PAIRS])
    q_copy = pltpu.make_async_copy(q_ref.at[0], qV, in_sem.at[3 * PAIRS + 1])
    k_copy.start()
    q_copy.start()

    def in_copy(p, which):
        ref, buf = ((x_ref, xV), (rate_ref, rV), (g_ref, gV))[which]
        lanes = pl.ds(pl.multiple_of(p * WIDE, WIDE), WIDE)
        return pltpu.make_async_copy(ref.at[0, :, lanes], buf.at[p], in_sem.at[p * 3 + which])

    for it in range(PAIRS):
        for which in range(3):
            in_copy(first_order(it), which).start()

    row = lax.broadcasted_iota(jnp.int32, (TOKENS, TOKENS), 0)
    col = lax.broadcasted_iota(jnp.int32, (TOKENS, TOKENS), 1)
    perm = jnp.where(col == (row % SEG) * LEN + row // SEG, 1.0, 0.0).astype(BF16)
    state_row = lax.broadcasted_iota(jnp.int32, (N, LANES), 0)
    state_col = lax.broadcasted_iota(jnp.int32, (N, LANES), 1)
    k_copy.wait()
    q_copy.wait()
    last = (((1,), (1,)), ((), ()))
    kp = lax.dot_general(perm, kV[...], last, preferred_element_type=F32).astype(BF16)
    qp = lax.dot_general(perm, qV[...], last, preferred_element_type=F32).astype(BF16)
    kL[...] = jnp.dot(kp, jnp.where(state_row == state_col, 1.0, 0.0).astype(BF16), preferred_element_type=F32)
    norm = jnp.zeros((TOKENS, LANES), F32)
    for n in range(N):
        pick = jnp.where(state_row == n, 1.0, 0.0).astype(BF16)
        kn = jnp.dot(kp, pick, preferred_element_type=F32)
        qn = jnp.dot(qp, pick, preferred_element_type=F32)
        k2 = kn * kn
        norm = norm + k2
        for i in range(LEN):
            kT[i * N + n] = kn[i * SEG:(i + 1) * SEG]
            k2T[i * N + n] = k2[i * SEG:(i + 1) * SEG]
            qT[i * N + n] = qn[i * SEG:(i + 1) * SEG]
    for i in range(LEN):
        knT[i] = norm[i * SEG:(i + 1) * SEG]

    def to_sibling(p, a):
        return pltpu.make_async_remote_copy(
            src_ref=send1.at[pl.ds(p * 4, 4)], dst_ref=recvC.at[pl.ds(a * 4, 4)], send_sem=c1_send.at[a],
            recv_sem=c1_recv.at[a], device_id={"ctx": sibling}, device_id_type=MESH)

    def to_owner(t):
        return pltpu.make_async_remote_copy(
            src_ref=send2.at[t], dst_ref=recv2.at[chip], send_sem=s2_sem.at[t], recv_sem=r2_sem.at[chip],
            device_id={"ctx": 2 * t + core}, device_id_type=MESH)

    def from_chip(t):
        return pltpu.make_async_remote_copy(
            src_ref=send2.at[t], dst_ref=recv2.at[t], send_sem=s2_sem.at[t], recv_sem=r2_sem.at[t],
            device_id={"ctx": 2 * t + core}, device_id_type=MESH)

    def to_chip(t):
        return pltpu.make_async_remote_copy(
            src_ref=send3.at[t], dst_ref=recv3.at[chip], send_sem=s3_sem.at[t], recv_sem=r3_sem.at[chip],
            device_id={"ctx": 2 * t + core}, device_id_type=MESH)

    def from_owner(t):
        return pltpu.make_async_remote_copy(
            src_ref=send3.at[t], dst_ref=recv3.at[t], send_sem=s3_sem.at[t], recv_sem=r3_sem.at[t],
            device_id={"ctx": 2 * t + core}, device_id_type=MESH)

    def entries_out(p, a):
        return pltpu.make_async_remote_copy(
            src_ref=sendS.at[pl.ds(a * 4, 4)], dst_ref=entry.at[pl.ds(p * 4, 4)], send_sem=c4_send.at[a],
            recv_sem=c4_recv.at[a], device_id={"ctx": sibling}, device_id_type=MESH)

    def both(p, a, j, which):
        mine = send1[p * 4 + j, which]
        other = recvC[a * 4 + j, which]
        return jnp.where(core == 0, mine, other), jnp.where(core == 0, other, mine)

    def join(p, a):
        to_sibling(p, a).wait_recv()
        for j in range(4):
            t = a * 4 + j
            p0, p1 = both(p, a, j, 0)
            l0, l1 = both(p, a, j, 1)
            b0, b1 = both(p, a, j, 2)
            send2[t, 0] = p0 * p1
            send2[t, 1] = l0 * p1 + l1
            send2[t, 2] = b0 + p0 * b1

            @pl.when(t != chip)
            def _():
                to_owner(t).start()

            @pl.when(t == chip)
            def _():
                recv2[t] = send2[t]

    def own_scan():
        for d in range(1, CHIPS):
            from_chip(lax.rem(chip + d, CHIPS)).wait_recv()
        state = jnp.zeros((SEG, LANES), F32)
        grad = state
        for c in range(CHIPS):
            send3[c, 0] = state
            state = state * recv2[c, 0] + recv2[c, 1]
        for c in reversed(range(CHIPS)):
            send3[c, 1] = grad
            grad = grad * recv2[c, 0] + recv2[c, 2]
        for d in sorted(range(1, CHIPS), key=lambda d: min(d, CHIPS - d)):
            to_chip(lax.rem(chip + d, CHIPS)).start()
        recv3[chip] = send3[chip]

    def split(p, a):
        for j in range(4):
            t = a * 4 + j

            @pl.when(t != chip)
            def _():
                from_owner(t).wait_recv()

            s0 = recv3[t, 0]
            g1 = recv3[t, 1]
            p0, p1 = both(p, a, j, 0)
            l0, _ = both(p, a, j, 1)
            _, b1 = both(p, a, j, 2)
            s1 = s0 * p0 + l0
            g0 = g1 * p1 + b1
            entry[p * 4 + j, 0] = jnp.where(core == 0, s0, s1)
            entry[p * 4 + j, 1] = jnp.where(core == 0, g0, g1)
            sendS[t, 0] = jnp.where(core == 0, s1, s0)
            sendS[t, 1] = jnp.where(core == 0, g1, g0)
        entries_out(p, a).start()

    def first_pass(it, _):
        p = first_order(it)
        for which in range(3):
            in_copy(p, which).wait()
        for c in range(2):
            lanes = pl.ds(c * LANES, LANES)
            x32[c] = xV[p, :, lanes].astype(F32)
            g32[c] = gV[p, :, lanes].astype(F32)
            r32[c] = rV[p, :, lanes]
        base = p * (2 * LEN)
        for i in range(LEN):
            for c in range(2):
                at = base + 2 * i + c
                rate = r32[c, pl.ds(i, SEG, stride=LEN), :]
                xv = x32[c, pl.ds(i, SEG, stride=LEN), :]
                gv = g32[c, pl.ds(i, SEG, stride=LEN), :]
                inv = 1.0 / (1.0 + rate * knT[i])
                step = rate * inv
                stepP[at] = step
                invP[at] = inv
                uP[at] = step * xv
                xP[at] = xv
                gP[at] = gv

        def n_group(ng, _):
            n0 = ng * 4
            prod = [None] * 8
            end = [None] * 8
            back = [None] * 8
            for i in range(LEN):
                step = [stepP[base + 2 * i + c] for c in range(2)]
                u = [uP[base + 2 * i + c] for c in range(2)]
                gv = [gP[base + 2 * i + c] for c in range(2)]
                for a in range(4):
                    kk = kT[i * N + n0 + a]
                    k2 = k2T[i * N + n0 + a]
                    qq = qT[i * N + n0 + a]
                    for c in range(2):
                        j = 2 * a + c
                        dec = 1.0 - step[c] * k2
                        decS[(p * LEN + i) * (2 * N) + 2 * n0 + j] = dec
                        emit = gv[c] * qq
                        drive = u[c] * kk
                        if i == 0:
                            prod[j] = dec
                            end[j] = drive
                            back[j] = emit * dec
                        else:
                            prod[j] = prod[j] * dec
                            end[j] = end[j] * dec + drive
                            back[j] = back[j] + emit * prod[j]
            for a in range(4):
                for c in range(2):
                    at = pl.multiple_of((c * N + n0 + a) * SEG, SEG)
                    sumP[pl.ds(at, SEG), :] = prod[2 * a + c]
                    sumL[pl.ds(at, SEG), :] = end[2 * a + c]
                    sumB[pl.ds(at, SEG), :] = back[2 * a + c]
            return 0

        lax.fori_loop(0, N // 4, n_group, 0)

        for j in range(4):
            o = p * 4 + j
            tile = j * 8 * SEG
            run_p = jnp.ones((SEG, LANES), F32)
            run_l = jnp.zeros((SEG, LANES), F32)
            ps, bs = [], []
            for s in range(SEG):
                pv = sumP[pl.ds(tile + s, SEG, stride=SEG), :]
                lv = sumL[pl.ds(tile + s, SEG, stride=SEG), :]
                ps.append(pv)
                bs.append(sumB[pl.ds(tile + s, SEG, stride=SEG), :])
                preP[o * SEG + s] = run_p
                preL[o * SEG + s] = run_l
                run_l = run_l * pv + lv
                run_p = run_p * pv
            send1[o, 0] = run_p
            send1[o, 1] = run_l
            run_p = jnp.ones((SEG, LANES), F32)
            run_b = jnp.zeros((SEG, LANES), F32)
            for s in reversed(range(SEG)):
                postP[o * SEG + s] = run_p
                postB[o * SEG + s] = run_b
                run_b = run_b * ps[s] + bs[s]
                run_p = run_p * ps[s]
            send1[o, 2] = run_b

        a = lax.rem(near + 1 + it, 2)

        @pl.when(it == 1)
        def _():
            pl.semaphore_wait(barrier, CHIPS + heads - 1)
            for b in range(2):
                to_sibling(2 * (1 - core) + b, b).start()

        @pl.when(it >= 2)
        def _():
            join(p, a)
        return 0

    lax.fori_loop(0, PAIRS, first_pass, 0)

    zero = jnp.zeros((SEG, LANES), F32)

    def clear(i, _):
        for n in range(N):
            accQ[i * N + n] = zero
            accK[i * N + n] = zero
        accN[i] = zero
        return 0

    lax.fori_loop(0, LEN, clear, 0)

    own_scan()

    def head_copy(p, h, owner, src_buf, dst, ssem, rsem):
        return pltpu.make_async_remote_copy(
            src_ref=src_buf.at[p, pl.ds(pl.multiple_of(h * rows_out, rows_out), rows_out), :],
            dst_ref=dst.at[0, :, pl.ds(pl.multiple_of(owner * (PAIRS * WIDE) + p * WIDE, WIDE), WIDE)],
            send_sem=ssem.at[p, h], recv_sem=rsem.at[p, owner],
            device_id={"head": h}, device_id_type=MESH)

    def own_copy(p, which, src_buf, dst):
        return pltpu.make_async_copy(
            src_buf.at[p, pl.ds(pl.multiple_of(hd * rows_out, rows_out), rows_out), :],
            dst.at[0, :, pl.ds(pl.multiple_of(hd * (PAIRS * WIDE) + p * WIDE, WIDE), WIDE)],
            own_sem.at[p, which])

    arrays = ((sendI, oi_ref, hi_send, hi_recv), (sendR, or_ref, hr_send, hr_recv))

    def second_pass(it, _):
        a = lax.rem(near + it, 2)
        p = 2 * lax.rem(core + it // 2, 2) + a
        base = p * (2 * LEN)

        @pl.when(it < 2)
        def _():
            split(p, a)

        @pl.when(it >= 2)
        def _():
            entries_out(p, a).wait_recv()

        for j in range(4):
            o = p * 4 + j
            s0 = entry[o, 0]
            g0 = entry[o, 1]
            tile = j * 8 * SEG
            for s in range(SEG):
                at = o * SEG + s
                sIn[pl.ds(tile + s, SEG, stride=SEG), :] = preP[at] * s0 + preL[at]
                gIn[pl.ds(tile + s, SEG, stride=SEG), :] = postP[at] * g0 + postB[at]

        def forward(i, states):
            states = list(states)
            u = [uP[base + 2 * i + c] for c in range(2)]
            gv = [gP[base + 2 * i + c] for c in range(2)]
            for n in range(N):
                kk = kT[i * N + n]
                total = accQ[i * N + n]
                for c in range(2):
                    j = n * 2 + c
                    kpS[i * (2 * N) + j] = kk * states[j]
                    states[j] = decS[(p * LEN + i) * (2 * N) + j] * states[j] + u[c] * kk
                    total = total + gv[c] * states[j]
                accQ[i * N + n] = total
            return tuple(states)

        start = tuple(sIn[pl.ds((c * N + n) * SEG, SEG), :] for n in range(N) for c in range(2))
        def forward_some(b, states):
            for r in range(STEPS):
                states = forward(b * STEPS + r, states)
            return states

        lax.fori_loop(0, LEN // STEPS, forward_some, start)

        def backward(it2, grads):
            i = LEN - 1 - it2
            grads = list(grads)
            step = [stepP[base + 2 * i + c] for c in range(2)]
            twice = [s + s for s in step]
            u = [uP[base + 2 * i + c] for c in range(2)]
            gv = [gP[base + 2 * i + c] for c in range(2)]
            key_dot = [None, None]
            weighted = [None, None]
            for n in range(N):
                kk = kT[i * N + n]
                qq = qT[i * N + n]
                total = accK[i * N + n]
                for c in range(2):
                    j = n * 2 + c
                    kprev = kpS[i * (2 * N) + j]
                    grad = grads[j] + gv[c] * qq
                    gk = grad * kk
                    wk = gk * kprev
                    key_dot[c] = gk if n == 0 else key_dot[c] + gk
                    weighted[c] = wk if n == 0 else weighted[c] + wk
                    total = total + grad * (u[c] - twice[c] * kprev)
                    grads[j] = grad * decS[(p * LEN + i) * (2 * N) + j]
                accK[i * N + n] = total
            norm_sum = accN[i]
            for c in range(2):
                at = base + 2 * i + c
                inv = invP[at]
                outI[c, pl.ds(i, SEG, stride=LEN), :] = step[c] * key_dot[c]
                grad_step = xP[at] * key_dot[c] - weighted[c]
                outR[c, pl.ds(i, SEG, stride=LEN), :] = grad_step * (inv * inv)
                norm_sum = norm_sum + grad_step * (step[c] * step[c])
            accN[i] = norm_sum
            return tuple(grads)

        start = tuple(gIn[pl.ds((c * N + n) * SEG, SEG), :] for n in range(N) for c in range(2))
        def backward_some(b, grads):
            for r in range(STEPS):
                grads = backward(b * STEPS + r, grads)
            return grads

        lax.fori_loop(0, LEN // STEPS, backward_some, start)
        for c in range(2):
            lanes = pl.ds(c * LANES, LANES)
            sendI[p, :, lanes] = outI[c].astype(BF16)
            sendR[p, :, lanes] = outR[c].astype(BF16)
        for d in range(1, heads):
            for src_buf, dst, ssem, rsem in arrays:
                head_copy(p, lax.rem(hd + d, heads), hd, src_buf, dst, ssem, rsem).start()
        own_copy(p, 0, sendI, oi_ref).start()
        own_copy(p, 1, sendR, or_ref).start()
        return 0

    lax.fori_loop(0, PAIRS, second_pass, 0)

    ones = jnp.ones((2 * LANES, LANES), BF16)
    lane = lax.broadcasted_iota(jnp.int32, (TOKENS, LANES), 1)

    def lane_sums(parts):
        whole = jnp.concatenate(parts, axis=0)
        high = whole.astype(BF16)
        low = (whole - high.astype(F32)).astype(BF16)
        return jnp.dot(jnp.concatenate([high, low], axis=1), ones, preferred_element_type=F32)

    merged = lane_sums([accN[i] for i in range(LEN)]) * (-2.0 * kL[...])
    for n in range(N):
        merged = jnp.where(lane == n, merged + lane_sums([accK[i * N + n] for i in range(LEN)]), merged)
        merged = jnp.where(lane == N + n, lane_sums([accQ[i * N + n] for i in range(LEN)]), merged)
    for i in range(LEN):
        sums[pl.ds(i, SEG, stride=LEN), :] = merged[i * SEG:(i + 1) * SEG]

    def sum_copy(h, src):
        return pltpu.make_async_remote_copy(
            src_ref=sums.at[pl.ds(pl.multiple_of(h * rows_out, rows_out), rows_out), :], dst_ref=rs_ref.at[src], send_sem=rs_send.at[h], recv_sem=rs_recv.at[src],
            device_id={"head": h}, device_id_type=MESH)

    for d in range(1, heads):
        sum_copy(lax.rem(hd + d, heads), hd).start()
    rs_ref[hd] = sums[pl.ds(pl.multiple_of(hd * rows_out, rows_out), rows_out), :]

    for d in range(1, CHIPS):
        to_owner(lax.rem(chip + d, CHIPS)).wait_send()
        to_chip(lax.rem(chip + d, CHIPS)).wait_send()
    for a in range(2):
        to_sibling(a, a).wait_send()
        entries_out(a, a).wait_send()
    for p in range(PAIRS):
        own_copy(p, 0, sendI, oi_ref).wait()
        own_copy(p, 1, sendR, or_ref).wait()
        for d in range(1, heads):
            h = lax.rem(hd + d, heads)
            for src_buf, dst, ssem, rsem in arrays:
                copy = head_copy(p, h, h, src_buf, dst, ssem, rsem)
                copy.wait_send()
                copy.wait_recv()
    for d in range(1, heads):
        h = lax.rem(hd + d, heads)
        copy = sum_copy(h, h)
        copy.wait_send()
        copy.wait_recv()


def finish(heads, i_ref, r_ref, s_ref, oi_ref, or_ref, ok_ref, oq_ref, small, sem):
    first = pltpu.make_async_copy(i_ref, oi_ref, sem.at[0])
    second = pltpu.make_async_copy(r_ref, or_ref, sem.at[1])
    first.start()
    second.start()
    total = s_ref[0]
    for h in range(1, heads):
        total = total + s_ref[h]
    turned = total.T
    small[0] = turned[:N]
    small[1] = turned[N:2 * N]
    third = pltpu.make_async_copy(small.at[0], ok_ref.at[0], sem.at[2])
    fourth = pltpu.make_async_copy(small.at[1], oq_ref.at[0], sem.at[3])
    third.start()
    fourth.start()
    for copy in (first, second, third, fourth):
        copy.wait()


def shards(heads):
    def run(inputs, step_rate, key_rows, query_rows, grad_out):
        rows_out = TOKENS // heads
        width = heads * PAIRS * WIDE
        vmem = pl.BlockSpec(memory_space=pltpu.VMEM)
        hbm = pl.BlockSpec(memory_space=pltpu.HBM)
        tile = (SEG, LANES)

        def regs(*lead):
            return pltpu.VMEM(lead + tile, F32)

        dma = pltpu.SemaphoreType.DMA
        wide = jax.ShapeDtypeStruct((1, rows_out, width), BF16)
        small = jax.ShapeDtypeStruct((1, N, rows_out), F32)
        grads_in, grads_rate, partial = pl.pallas_call(
            lambda *refs: kernel(heads, *refs),
            out_shape=(
                pltpu.VMEM((1, rows_out, width), BF16),
                pltpu.VMEM((1, rows_out, width), BF16),
                pltpu.VMEM((heads, rows_out, LANES), F32),
            ),
            in_specs=[hbm] * 5,
            out_specs=(vmem, vmem, vmem),
            scratch_shapes=[
                pltpu.VMEM((PAIRS, TOKENS, WIDE), BF16), pltpu.VMEM((PAIRS, TOKENS, WIDE), F32),
                pltpu.VMEM((PAIRS, TOKENS, WIDE), BF16),
                pltpu.VMEM((N, TOKENS), BF16), pltpu.VMEM((N, TOKENS), BF16),
                regs(LEN * N), regs(LEN * N), regs(LEN * N), regs(LEN), pltpu.VMEM((TOKENS, LANES), F32),
                *[pltpu.VMEM((2, TOKENS, LANES), F32) for _ in range(3)],
                *[regs(PAIRS * 2 * LEN) for _ in range(5)],
                regs(PAIRS * LEN * 2 * N),
                *[pltpu.VMEM((2 * N * SEG, LANES), F32) for _ in range(3)],
                *[regs(CTX * SEG) for _ in range(4)],
                regs(CTX, 3), regs(CHIPS, 3), regs(CHIPS, 3), regs(CHIPS, 3),
                regs(CHIPS, 2), regs(CHIPS, 2), regs(CHIPS, 2), regs(CTX, 2),
                pltpu.VMEM((2 * N * SEG, LANES), F32), pltpu.VMEM((2 * N * SEG, LANES), F32),
                regs(LEN * 2 * N),
                regs(LEN * N), regs(LEN * N), regs(LEN),
                pltpu.VMEM((2, TOKENS, LANES), F32), pltpu.VMEM((2, TOKENS, LANES), F32),
                pltpu.VMEM((PAIRS, TOKENS, WIDE), BF16), pltpu.VMEM((PAIRS, TOKENS, WIDE), BF16),
                pltpu.VMEM((TOKENS, LANES), F32),
                dma((3 * PAIRS + 2,)),
                dma((2,)), dma((2,)), *[dma((CHIPS,)) for _ in range(4)], dma((2,)), dma((2,)),
                dma((PAIRS, heads)), dma((PAIRS, heads)), dma((PAIRS, heads)), dma((PAIRS, heads)),
                dma((PAIRS, 2)), dma((heads,)), dma((heads,)),
            ],
            compiler_params=pltpu.CompilerParams(
                collective_id=0, has_side_effects=True, vmem_limit_bytes=48 * 1024 * 1024),
        )(*(
            pltpu.with_memory_space_constraint(a, pltpu.HBM)
            for a in (inputs, step_rate, jnp.swapaxes(key_rows, 1, 2), jnp.swapaxes(query_rows, 1, 2), grad_out)
        ))
        grads_in, grads_rate, keys, queries = pl.pallas_call(
            lambda *refs: finish(heads, *refs),
            out_shape=(wide, wide, small, small),
            in_specs=[vmem, vmem, vmem],
            out_specs=(hbm, hbm, hbm, hbm),
            scratch_shapes=[pltpu.VMEM((2, N, rows_out), F32), dma((4,))],
        )(*(pltpu.with_memory_space_constraint(a, pltpu.VMEM) for a in (grads_in, grads_rate, partial)))
        return grads_in, grads_rate, jnp.swapaxes(keys, 1, 2), jnp.swapaxes(queries, 1, 2)

    return run


def solution(mesh):
    placed = (
        P("dp", "ctx", "head"),
        P("dp", "ctx", "head"),
        P("dp", "ctx", None),
        P("dp", "ctx", None),
        P("dp", "ctx", "head"),
    )
    out = P("dp", ("ctx", "head"), None)
    return jax.shard_map(
        shards(mesh.shape["head"]),
        mesh=mesh,
        in_specs=placed,
        out_specs=(out, out, out, out),
        check_vma=False,
    )
```

```python
import jax
import jax.numpy as jnp
from jax import lax
from jax.experimental import pallas as pl
from jax.experimental.pallas import tpu as pltpu
from jax.sharding import PartitionSpec as P

MESH = pl.DeviceIdType.MESH
F32 = jnp.float32
BF16 = jnp.bfloat16

SEG = 8
LEN = 16
N = 16
LANES = 128
PAIRS = 4
WIDE = 256
CTX = 16
CHIPS = CTX // 2
STEPS = 4
TOKENS = SEG * LEN


def kernel(
    heads,
    x_ref, rate_ref, k_ref, q_ref, g_ref,
    o_ref, rs_ref,
    xV, rV, gV, kV, qV,
    kT, k2T, qT, knT, kL,
    x32, g32, r32,
    stepP, uP, gP, xP, invP, decS, driveS, emitS,
    sumP, sumL, sumB,
    preP, preL, postP, postB,
    send1, recvC, send2, recv2, send3, recv3, sendS, entry,
    sIn, gIn, kpS,
    accQ, accK, accN,
    outI, outR, sendB,
    sums,
    in_sem, c1_send, c1_recv, s2_sem, r2_sem, s3_sem, r3_sem, c4_send, c4_recv,
    h_send, h_recv, own_sem, rs_send, rs_recv,
):
    me = lax.axis_index("ctx")
    hd = lax.axis_index("head")
    rows_out = TOKENS // heads
    chip = me // 2
    core = lax.rem(me, 2)
    sibling = me + 1 - 2 * core
    near = chip // 4

    def on_chip(d):
        return 2 * lax.rem(chip + d, CHIPS) + core

    barrier = pltpu.get_barrier_semaphore()
    for d in sorted(range(1, CHIPS), key=lambda d: -min(d, CHIPS - d)):
        pl.semaphore_signal(barrier, inc=1, device_id={"ctx": on_chip(d)}, device_id_type=MESH)
    for d in range(1, heads):
        pl.semaphore_signal(barrier, inc=1, device_id={"head": lax.rem(hd + d, heads)}, device_id_type=MESH)
    pl.semaphore_signal(barrier, inc=1, device_id={"ctx": sibling}, device_id_type=MESH)

    def first_order(it):
        return 2 * lax.rem(core + 1 + it // 2, 2) + lax.rem(near + 1 + it, 2)

    k_copy = pltpu.make_async_copy(k_ref.at[0], kV, in_sem.at[3 * PAIRS])
    q_copy = pltpu.make_async_copy(q_ref.at[0], qV, in_sem.at[3 * PAIRS])
    k_copy.start()
    q_copy.start()

    def in_copy(p, which):
        ref, buf = ((x_ref, xV), (rate_ref, rV), (g_ref, gV))[which]
        lanes = pl.ds(pl.multiple_of(p * WIDE, WIDE), WIDE)
        return pltpu.make_async_copy(ref.at[0, :, lanes], buf.at[p], in_sem.at[p * 3 + which])

    for it in range(PAIRS):
        for which in range(3):
            in_copy(first_order(it), which).start()

    row = lax.broadcasted_iota(jnp.int32, (TOKENS, TOKENS), 0)
    col = lax.broadcasted_iota(jnp.int32, (TOKENS, TOKENS), 1)
    perm = jnp.where(col == (row % SEG) * LEN + row // SEG, 1.0, 0.0).astype(BF16)
    state_row = lax.broadcasted_iota(jnp.int32, (N, LANES), 0)
    state_col = lax.broadcasted_iota(jnp.int32, (N, LANES), 1)
    k_copy.wait()
    q_copy.wait()
    last = (((1,), (1,)), ((), ()))
    kp = lax.dot_general(perm, kV[...], last, preferred_element_type=F32).astype(BF16)
    qp = lax.dot_general(perm, qV[...], last, preferred_element_type=F32).astype(BF16)
    kL[...] = jnp.dot(kp, jnp.where(state_row == state_col, 1.0, 0.0).astype(BF16), preferred_element_type=F32)
    norm = jnp.zeros((TOKENS, LANES), F32)
    for n in range(N):
        pick = jnp.where(state_row == n, 1.0, 0.0).astype(BF16)
        kn = jnp.dot(kp, pick, preferred_element_type=F32)
        qn = jnp.dot(qp, pick, preferred_element_type=F32)
        k2 = kn * kn
        norm = norm + k2
        for i in range(LEN):
            kT[i * N + n] = kn[i * SEG:(i + 1) * SEG]
            k2T[i * N + n] = k2[i * SEG:(i + 1) * SEG]
            qT[i * N + n] = qn[i * SEG:(i + 1) * SEG]
    for i in range(LEN):
        knT[i] = norm[i * SEG:(i + 1) * SEG]

    def to_sibling(p, a):
        return pltpu.make_async_remote_copy(
            src_ref=send1.at[pl.ds(p * 4, 4)], dst_ref=recvC.at[pl.ds(a * 4, 4)], send_sem=c1_send.at[a],
            recv_sem=c1_recv.at[a], device_id={"ctx": sibling}, device_id_type=MESH)

    def to_owner(t):
        return pltpu.make_async_remote_copy(
            src_ref=send2.at[t], dst_ref=recv2.at[chip], send_sem=s2_sem.at[t], recv_sem=r2_sem.at[chip],
            device_id={"ctx": 2 * t + core}, device_id_type=MESH)

    def from_chip(t):
        return pltpu.make_async_remote_copy(
            src_ref=send2.at[t], dst_ref=recv2.at[t], send_sem=s2_sem.at[t], recv_sem=r2_sem.at[t],
            device_id={"ctx": 2 * t + core}, device_id_type=MESH)

    def to_chip(t):
        return pltpu.make_async_remote_copy(
            src_ref=send3.at[t], dst_ref=recv3.at[chip], send_sem=s3_sem.at[t], recv_sem=r3_sem.at[chip],
            device_id={"ctx": 2 * t + core}, device_id_type=MESH)

    def from_owner(t):
        return pltpu.make_async_remote_copy(
            src_ref=send3.at[t], dst_ref=recv3.at[t], send_sem=s3_sem.at[t], recv_sem=r3_sem.at[t],
            device_id={"ctx": 2 * t + core}, device_id_type=MESH)

    def entries_out(p, a):
        return pltpu.make_async_remote_copy(
            src_ref=sendS.at[pl.ds(a * 4, 4)], dst_ref=entry.at[pl.ds(p * 4, 4)], send_sem=c4_send.at[a],
            recv_sem=c4_recv.at[a], device_id={"ctx": sibling}, device_id_type=MESH)

    def both(p, a, j, which):
        mine = send1[p * 4 + j, which]
        other = recvC[a * 4 + j, which]
        return jnp.where(core == 0, mine, other), jnp.where(core == 0, other, mine)

    def join(p, a):
        to_sibling(p, a).wait_recv()
        for j in range(4):
            t = a * 4 + j
            p0, p1 = both(p, a, j, 0)
            l0, l1 = both(p, a, j, 1)
            b0, b1 = both(p, a, j, 2)
            send2[t, 0] = p0 * p1
            send2[t, 1] = l0 * p1 + l1
            send2[t, 2] = b0 + p0 * b1

            @pl.when(t != chip)
            def _():
                to_owner(t).start()

            @pl.when(t == chip)
            def _():
                recv2[t] = send2[t]

    def own_scan():
        for d in range(1, CHIPS):
            from_chip(lax.rem(chip + d, CHIPS)).wait_recv()
        state = jnp.zeros((SEG, LANES), F32)
        grad = state
        for c in range(CHIPS):
            send3[c, 0] = state
            state = state * recv2[c, 0] + recv2[c, 1]
        for c in reversed(range(CHIPS)):
            send3[c, 1] = grad
            grad = grad * recv2[c, 0] + recv2[c, 2]
        for d in sorted(range(1, CHIPS), key=lambda d: min(d, CHIPS - d)):
            to_chip(lax.rem(chip + d, CHIPS)).start()
        recv3[chip] = send3[chip]

    def split(p, a):
        for j in range(4):
            t = a * 4 + j

            @pl.when(t != chip)
            def _():
                from_owner(t).wait_recv()

            s0 = recv3[t, 0]
            g1 = recv3[t, 1]
            p0, p1 = both(p, a, j, 0)
            l0, _ = both(p, a, j, 1)
            _, b1 = both(p, a, j, 2)
            s1 = s0 * p0 + l0
            g0 = g1 * p1 + b1
            entry[p * 4 + j, 0] = jnp.where(core == 0, s0, s1)
            entry[p * 4 + j, 1] = jnp.where(core == 0, g0, g1)
            sendS[t, 0] = jnp.where(core == 0, s1, s0)
            sendS[t, 1] = jnp.where(core == 0, g1, g0)
        entries_out(p, a).start()

    def first_pass(it, _):
        p = first_order(it)
        for which in range(3):
            in_copy(p, which).wait()
        for c in range(2):
            lanes = pl.ds(c * LANES, LANES)
            x32[c] = xV[p, :, lanes].astype(F32)
            g32[c] = gV[p, :, lanes].astype(F32)
            r32[c] = rV[p, :, lanes]
        base = p * (2 * LEN)
        for i in range(LEN):
            for c in range(2):
                at = base + 2 * i + c
                rate = r32[c, pl.ds(i, SEG, stride=LEN), :]
                xv = x32[c, pl.ds(i, SEG, stride=LEN), :]
                gv = g32[c, pl.ds(i, SEG, stride=LEN), :]
                inv = 1.0 / (1.0 + rate * knT[i])
                step = rate * inv
                stepP[at] = step
                invP[at] = inv
                uP[at] = step * xv
                xP[at] = xv
                gP[at] = gv

        def n_group(ng, _):
            n0 = ng * 4
            prod = [None] * 8
            end = [None] * 8
            back = [None] * 8
            for i in range(LEN):
                step = [stepP[base + 2 * i + c] for c in range(2)]
                u = [uP[base + 2 * i + c] for c in range(2)]
                gv = [gP[base + 2 * i + c] for c in range(2)]
                for a in range(4):
                    kk = kT[i * N + n0 + a]
                    k2 = k2T[i * N + n0 + a]
                    qq = qT[i * N + n0 + a]
                    for c in range(2):
                        j = 2 * a + c
                        dec = 1.0 - step[c] * k2
                        decS[(p * LEN + i) * (2 * N) + 2 * n0 + j] = dec
                        emit = gv[c] * qq
                        drive = u[c] * kk
                        if i == 0:
                            prod[j] = dec
                            end[j] = drive
                            back[j] = emit * dec
                        else:
                            prod[j] = prod[j] * dec
                            end[j] = end[j] * dec + drive
                            back[j] = back[j] + emit * prod[j]
            for a in range(4):
                for c in range(2):
                    at = pl.multiple_of((c * N + n0 + a) * SEG, SEG)
                    sumP[pl.ds(at, SEG), :] = prod[2 * a + c]
                    sumL[pl.ds(at, SEG), :] = end[2 * a + c]
                    sumB[pl.ds(at, SEG), :] = back[2 * a + c]
            return 0

        lax.fori_loop(0, N // 4, n_group, 0)

        for j in range(4):
            o = p * 4 + j
            tile = j * 8 * SEG
            run_p = jnp.ones((SEG, LANES), F32)
            run_l = jnp.zeros((SEG, LANES), F32)
            ps, bs = [], []
            for s in range(SEG):
                pv = sumP[pl.ds(tile + s, SEG, stride=SEG), :]
                lv = sumL[pl.ds(tile + s, SEG, stride=SEG), :]
                ps.append(pv)
                bs.append(sumB[pl.ds(tile + s, SEG, stride=SEG), :])
                preP[o * SEG + s] = run_p
                preL[o * SEG + s] = run_l
                run_l = run_l * pv + lv
                run_p = run_p * pv
            send1[o, 0] = run_p
            send1[o, 1] = run_l
            run_p = jnp.ones((SEG, LANES), F32)
            run_b = jnp.zeros((SEG, LANES), F32)
            for s in reversed(range(SEG)):
                postP[o * SEG + s] = run_p
                postB[o * SEG + s] = run_b
                run_b = run_b * ps[s] + bs[s]
                run_p = run_p * ps[s]
            send1[o, 2] = run_b

        a = lax.rem(near + 1 + it, 2)

        @pl.when(it == 1)
        def _():
            pl.semaphore_wait(barrier, CHIPS + heads - 1)
            for b in range(2):
                to_sibling(2 * (1 - core) + b, b).start()

        @pl.when(it >= 2)
        def _():
            join(p, a)
        return 0

    lax.fori_loop(0, PAIRS, first_pass, 0)

    zero = jnp.zeros((SEG, LANES), F32)

    def clear(i, _):
        for n in range(N):
            accQ[i * N + n] = zero
            accK[i * N + n] = zero
        accN[i] = zero
        return 0

    lax.fori_loop(0, LEN, clear, 0)

    own_scan()

    def fill(at, _):
        i = lax.rem(at, LEN)
        u = [uP[2 * at + c] for c in range(2)]
        gv = [gP[2 * at + c] for c in range(2)]
        for n in range(N):
            kk = kT[i * N + n]
            qq = qT[i * N + n]
            for c in range(2):
                driveS[at * (2 * N) + 2 * n + c] = u[c] * kk
                emitS[at * (2 * N) + 2 * n + c] = gv[c] * qq
        return 0

    lax.fori_loop(0, PAIRS * LEN, fill, 0)

    def pair_at(it):
        return 2 * lax.rem(core + it // 2, 2) + lax.rem(near + it, 2)

    def part_lanes(p, c):
        return (pl.ds(0, WIDE), p * WIDE, WIDE) if c is None else (
            pl.ds(pl.multiple_of(c * LANES, LANES), LANES), p * WIDE + c * LANES, LANES)

    def head_copy(slot, p, c, h, owner):
        lanes, column, width = part_lanes(p, c)
        return pltpu.make_async_remote_copy(
            src_ref=sendB.at[p, :, pl.ds(pl.multiple_of(h * rows_out, rows_out), rows_out), lanes],
            dst_ref=o_ref.at[:, :, pl.ds(pl.multiple_of(owner * (PAIRS * WIDE) + column, width), width)],
            send_sem=h_send.at[slot, h], recv_sem=h_recv.at[slot, owner],
            device_id={"head": h}, device_id_type=MESH)

    def own_copy(slot, p, c):
        lanes, column, width = part_lanes(p, c)
        return pltpu.make_async_copy(
            sendB.at[p, :, pl.ds(pl.multiple_of(hd * rows_out, rows_out), rows_out), lanes],
            o_ref.at[:, :, pl.ds(pl.multiple_of(hd * (PAIRS * WIDE) + column, width), width)],
            own_sem.at[slot])

    def ship(slot, p, c):
        for d in sorted(range(1, heads), key=lambda d: -min(d, heads - d)):
            head_copy(slot, p, c, lax.rem(hd + d, heads), hd).start()
        own_copy(slot, p, c).start()

    def shipped(slot, p, c):
        own_copy(slot, p, c).wait()
        for d in range(1, heads):
            h = lax.rem(hd + d, heads)
            copy = head_copy(slot, p, c, h, h)
            copy.wait_send()
            copy.wait_recv()

    def second_pass(it):
        a = lax.rem(near + it, 2)
        p = 2 * lax.rem(core + it // 2, 2) + a
        base = p * (2 * LEN)

        @pl.when(it < 2)
        def _():
            split(p, a)

        @pl.when(it >= 2)
        def _():
            entries_out(p, a).wait_recv()

        for j in range(4):
            o = p * 4 + j
            s0 = entry[o, 0]
            g0 = entry[o, 1]
            tile = j * 8 * SEG
            for s in range(SEG):
                at = o * SEG + s
                sIn[pl.ds(tile + s, SEG, stride=SEG), :] = preP[at] * s0 + preL[at]
                gIn[pl.ds(tile + s, SEG, stride=SEG), :] = postP[at] * g0 + postB[at]

        return p, base

    def grads_of(p, base, chunks):
        width = len(chunks)

        def forward(i, states):
            states = list(states)
            gv = [gP[base + 2 * i + c] for c in chunks]
            for n in range(N):
                kk = kT[i * N + n]
                total = accQ[i * N + n]
                for b, c in enumerate(chunks):
                    j = n * width + b
                    kpS[i * (2 * N) + j] = kk * states[j]
                    states[j] = decS[(p * LEN + i) * (2 * N) + 2 * n + c] * states[j] + driveS[(p * LEN + i) * (2 * N) + 2 * n + c]
                    total = total + gv[b] * states[j]
                accQ[i * N + n] = total
            return tuple(states)

        def forward_some(b, states):
            for r in range(STEPS):
                states = forward(b * STEPS + r, states)
            return states

        def start(ref):
            return tuple(
                ref[pl.ds(pl.multiple_of((c * N + n) * SEG, SEG), SEG), :] for n in range(N) for c in chunks)

        lax.fori_loop(0, LEN // STEPS, forward_some, start(sIn))

        def backward(it2, grads):
            i = LEN - 1 - it2
            grads = list(grads)
            step = [stepP[base + 2 * i + c] for c in chunks]
            twice = [s + s for s in step]
            u = [uP[base + 2 * i + c] for c in chunks]
            key_dot = [None] * width
            weighted = [None] * width
            for n in range(N):
                kk = kT[i * N + n]
                total = accK[i * N + n]
                for b, c in enumerate(chunks):
                    j = n * width + b
                    kprev = kpS[i * (2 * N) + j]
                    grad = grads[j] + emitS[(p * LEN + i) * (2 * N) + 2 * n + c]
                    gk = grad * kk
                    wk = gk * kprev
                    key_dot[b] = gk if n == 0 else key_dot[b] + gk
                    weighted[b] = wk if n == 0 else weighted[b] + wk
                    total = total + grad * (u[b] - twice[b] * kprev)
                    grads[j] = grad * decS[(p * LEN + i) * (2 * N) + 2 * n + c]
                accK[i * N + n] = total
            norm_sum = accN[i]
            for b, c in enumerate(chunks):
                at = base + 2 * i + c
                inv = invP[at]
                outI[b, pl.ds(i, SEG, stride=LEN), :] = step[b] * key_dot[b]
                grad_step = xP[at] * key_dot[b] - weighted[b]
                outR[b, pl.ds(i, SEG, stride=LEN), :] = grad_step * (inv * inv)
                norm_sum = norm_sum + grad_step * (step[b] * step[b])
            accN[i] = norm_sum
            return tuple(grads)

        def backward_some(b, grads):
            for r in range(STEPS):
                grads = backward(b * STEPS + r, grads)
            return grads

        lax.fori_loop(0, LEN // STEPS, backward_some, start(gIn))
        for b, c in enumerate(chunks):
            lanes = pl.ds(c * LANES, LANES) if isinstance(c, int) else pl.ds(pl.multiple_of(c * LANES, LANES), LANES)
            sendB[p, 0, :, lanes] = outI[b].astype(BF16)
            sendB[p, 1, :, lanes] = outR[b].astype(BF16)

    def pair_grads(it, _):
        p, base = second_pass(it)
        grads_of(p, base, (0, 1))
        ship(it, p, None)
        return 0

    lax.fori_loop(0, PAIRS, pair_grads, 0)

    ones = jnp.ones((2 * LANES, LANES), BF16)
    lane = lax.broadcasted_iota(jnp.int32, (TOKENS, LANES), 1)

    def lane_sums(parts):
        whole = jnp.concatenate(parts, axis=0)
        high = whole.astype(BF16)
        low = (whole - high.astype(F32)).astype(BF16)
        return jnp.dot(jnp.concatenate([high, low], axis=1), ones, preferred_element_type=F32)

    merged = lane_sums([accN[i] for i in range(LEN)]) * (-2.0 * kL[...])
    for n in range(N):
        merged = jnp.where(lane == n, merged + lane_sums([accK[i * N + n] for i in range(LEN)]), merged)
        merged = jnp.where(lane == N + n, lane_sums([accQ[i * N + n] for i in range(LEN)]), merged)
    for i in range(LEN):
        sums[pl.ds(i, SEG, stride=LEN), :] = merged[i * SEG:(i + 1) * SEG]

    def sum_copy(h, src):
        return pltpu.make_async_remote_copy(
            src_ref=sums.at[pl.ds(pl.multiple_of(h * rows_out, rows_out), rows_out), :], dst_ref=rs_ref.at[src], send_sem=rs_send.at[h], recv_sem=rs_recv.at[src],
            device_id={"head": h}, device_id_type=MESH)

    for d in range(1, heads):
        sum_copy(lax.rem(hd + d, heads), hd).start()
    rs_ref[hd] = sums[pl.ds(pl.multiple_of(hd * rows_out, rows_out), rows_out), :]

    for d in range(1, CHIPS):
        to_owner(lax.rem(chip + d, CHIPS)).wait_send()
        to_chip(lax.rem(chip + d, CHIPS)).wait_send()
    for a in range(2):
        to_sibling(a, a).wait_send()
        entries_out(a, a).wait_send()
    for it in range(PAIRS):
        shipped(it, pair_at(it), None)
    for d in range(1, heads):
        h = lax.rem(hd + d, heads)
        copy = sum_copy(h, h)
        copy.wait_send()
        copy.wait_recv()


def finish(heads, b_ref, s_ref, oi_ref, or_ref, ok_ref, oq_ref, small, sem):
    first = pltpu.make_async_copy(b_ref.at[pl.ds(0, 1)], oi_ref, sem.at[0])
    second = pltpu.make_async_copy(b_ref.at[pl.ds(1, 1)], or_ref, sem.at[1])
    first.start()
    second.start()
    total = s_ref[0]
    for h in range(1, heads):
        total = total + s_ref[h]
    turned = total.T
    small[0] = turned[:N]
    small[1] = turned[N:2 * N]
    third = pltpu.make_async_copy(small.at[0], ok_ref.at[0], sem.at[2])
    fourth = pltpu.make_async_copy(small.at[1], oq_ref.at[0], sem.at[3])
    third.start()
    fourth.start()
    for copy in (first, second, third, fourth):
        copy.wait()


def shards(heads):
    def run(inputs, step_rate, key_rows, query_rows, grad_out):
        rows_out = TOKENS // heads
        width = heads * PAIRS * WIDE
        vmem = pl.BlockSpec(memory_space=pltpu.VMEM)
        hbm = pl.BlockSpec(memory_space=pltpu.HBM)
        tile = (SEG, LANES)

        def regs(*lead):
            return pltpu.VMEM(lead + tile, F32)

        dma = pltpu.SemaphoreType.DMA
        wide = jax.ShapeDtypeStruct((1, rows_out, width), BF16)
        small = jax.ShapeDtypeStruct((1, N, rows_out), F32)
        grads, partial = pl.pallas_call(
            lambda *refs: kernel(heads, *refs),
            out_shape=(
                pltpu.VMEM((2, rows_out, width), BF16),
                pltpu.VMEM((heads, rows_out, LANES), F32),
            ),
            in_specs=[hbm] * 5,
            out_specs=(vmem, vmem),
            scratch_shapes=[
                pltpu.VMEM((PAIRS, TOKENS, WIDE), BF16), pltpu.VMEM((PAIRS, TOKENS, WIDE), F32),
                pltpu.VMEM((PAIRS, TOKENS, WIDE), BF16),
                pltpu.VMEM((N, TOKENS), BF16), pltpu.VMEM((N, TOKENS), BF16),
                regs(LEN * N), regs(LEN * N), regs(LEN * N), regs(LEN), pltpu.VMEM((TOKENS, LANES), F32),
                *[pltpu.VMEM((2, TOKENS, LANES), F32) for _ in range(3)],
                *[regs(PAIRS * 2 * LEN) for _ in range(5)],
                regs(PAIRS * LEN * 2 * N),
                regs(PAIRS * LEN * 2 * N),
                regs(PAIRS * LEN * 2 * N),
                *[pltpu.VMEM((2 * N * SEG, LANES), F32) for _ in range(3)],
                *[regs(CTX * SEG) for _ in range(4)],
                regs(CTX, 3), regs(CHIPS, 3), regs(CHIPS, 3), regs(CHIPS, 3),
                regs(CHIPS, 2), regs(CHIPS, 2), regs(CHIPS, 2), regs(CTX, 2),
                pltpu.VMEM((2 * N * SEG, LANES), F32), pltpu.VMEM((2 * N * SEG, LANES), F32),
                regs(LEN * 2 * N),
                regs(LEN * N), regs(LEN * N), regs(LEN),
                pltpu.VMEM((2, TOKENS, LANES), F32), pltpu.VMEM((2, TOKENS, LANES), F32),
                pltpu.VMEM((PAIRS, 2, TOKENS, WIDE), BF16),
                pltpu.VMEM((TOKENS, LANES), F32),
                dma((3 * PAIRS + 2,)),
                dma((2,)), dma((2,)), *[dma((CHIPS,)) for _ in range(4)], dma((2,)), dma((2,)),
                dma((PAIRS, heads)), dma((PAIRS, heads)), dma((PAIRS,)), dma((heads,)), dma((heads,)),
            ],
            compiler_params=pltpu.CompilerParams(
                collective_id=0, has_side_effects=True, vmem_limit_bytes=48 * 1024 * 1024),
        )(*(
            pltpu.with_memory_space_constraint(a, pltpu.HBM)
            for a in (inputs, step_rate, jnp.swapaxes(key_rows, 1, 2), jnp.swapaxes(query_rows, 1, 2), grad_out)
        ))
        grads_in, grads_rate, keys, queries = pl.pallas_call(
            lambda *refs: finish(heads, *refs),
            out_shape=(wide, wide, small, small),
            in_specs=[vmem, vmem],
            out_specs=(hbm, hbm, hbm, hbm),
            scratch_shapes=[pltpu.VMEM((2, N, rows_out), F32), dma((4,))],
        )(*(pltpu.with_memory_space_constraint(a, pltpu.VMEM) for a in (grads, partial)))
        return grads_in, grads_rate, jnp.swapaxes(keys, 1, 2), jnp.swapaxes(queries, 1, 2)

    return run


def solution(mesh):
    placed = (
        P("dp", "ctx", "head"),
        P("dp", "ctx", "head"),
        P("dp", "ctx", None),
        P("dp", "ctx", None),
        P("dp", "ctx", "head"),
    )
    out = P("dp", ("ctx", "head"), None)
    return jax.shard_map(
        shards(mesh.shape["head"]),
        mesh=mesh,
        in_specs=placed,
        out_specs=(out, out, out, out),
        check_vma=False,
    )
```

```python
import jax
import jax.numpy as jnp
from jax import lax
from jax.experimental import pallas as pl
from jax.experimental.pallas import tpu as pltpu
from jax.sharding import PartitionSpec as P

MESH = pl.DeviceIdType.MESH
F32 = jnp.float32
BF16 = jnp.bfloat16

SEG = 8
LEN = 16
N = 16
LANES = 128
PAIRS = 4
WIDE = 256
CTX = 16
CHIPS = CTX // 2
STEPS = 4
TOKENS = SEG * LEN


def kernel(
    heads,
    x_ref, rate_ref, k_ref, q_ref, g_ref,
    o_ref, rs_ref,
    xV, rV, gV, kV, qV,
    kT, k2T, qT, knT, kL,
    x32, g32, r32,
    stepP, uP, gP, xP, invP, decS, driveS, emitS,
    sumP, sumL, sumB,
    preP, preL, postP, postB,
    send1, recvC, send2, recv2, send3, recv3, sendS, entry,
    sIn, gIn, kpS,
    accQ, accK, accN,
    outI, outR, sendB,
    sums, packS,
    in_sem, c1_send, c1_recv, s2_sem, r2_sem, s3_sem, r3_sem, c4_send, c4_recv,
    h_send, h_recv, own_sem, rs_send, rs_recv,
):
    me = lax.axis_index("ctx")
    hd = lax.axis_index("head")
    rows_out = TOKENS // heads
    chip = me // 2
    core = lax.rem(me, 2)
    sibling = me + 1 - 2 * core
    near = chip // 4

    def on_chip(d):
        return 2 * lax.rem(chip + d, CHIPS) + core

    barrier = pltpu.get_barrier_semaphore()
    for d in sorted(range(1, CHIPS), key=lambda d: -min(d, CHIPS - d)):
        pl.semaphore_signal(barrier, inc=1, device_id={"ctx": on_chip(d)}, device_id_type=MESH)
    for d in range(1, heads):
        pl.semaphore_signal(barrier, inc=1, device_id={"head": lax.rem(hd + d, heads)}, device_id_type=MESH)
    pl.semaphore_signal(barrier, inc=1, device_id={"ctx": sibling}, device_id_type=MESH)

    def first_order(it):
        return 2 * lax.rem(core + 1 + it // 2, 2) + lax.rem(near + 1 + it, 2)

    k_copy = pltpu.make_async_copy(k_ref.at[0], kV, in_sem.at[3 * PAIRS])
    q_copy = pltpu.make_async_copy(q_ref.at[0], qV, in_sem.at[3 * PAIRS])
    k_copy.start()
    q_copy.start()

    def in_copy(p, which):
        ref, buf = ((x_ref, xV), (rate_ref, rV), (g_ref, gV))[which]
        lanes = pl.ds(pl.multiple_of(p * WIDE, WIDE), WIDE)
        return pltpu.make_async_copy(ref.at[0, :, lanes], buf.at[p], in_sem.at[p * 3 + which])

    for it in range(PAIRS):
        for which in range(3):
            in_copy(first_order(it), which).start()

    row = lax.broadcasted_iota(jnp.int32, (TOKENS, TOKENS), 0)
    col = lax.broadcasted_iota(jnp.int32, (TOKENS, TOKENS), 1)
    perm = jnp.where(col == (row % SEG) * LEN + row // SEG, 1.0, 0.0).astype(BF16)
    state_row = lax.broadcasted_iota(jnp.int32, (N, LANES), 0)
    state_col = lax.broadcasted_iota(jnp.int32, (N, LANES), 1)
    k_copy.wait()
    q_copy.wait()
    last = (((1,), (1,)), ((), ()))
    kp = lax.dot_general(perm, kV[...], last, preferred_element_type=F32).astype(BF16)
    qp = lax.dot_general(perm, qV[...], last, preferred_element_type=F32).astype(BF16)
    kL[...] = jnp.dot(kp, jnp.where(state_row == state_col, 1.0, 0.0).astype(BF16), preferred_element_type=F32)
    norm = jnp.zeros((TOKENS, LANES), F32)
    for n in range(N):
        pick = jnp.where(state_row == n, 1.0, 0.0).astype(BF16)
        kn = jnp.dot(kp, pick, preferred_element_type=F32)
        qn = jnp.dot(qp, pick, preferred_element_type=F32)
        k2 = kn * kn
        norm = norm + k2
        for i in range(LEN):
            kT[i * N + n] = kn[i * SEG:(i + 1) * SEG]
            k2T[i * N + n] = k2[i * SEG:(i + 1) * SEG]
            qT[i * N + n] = qn[i * SEG:(i + 1) * SEG]
    for i in range(LEN):
        knT[i] = norm[i * SEG:(i + 1) * SEG]

    def to_sibling(p, a):
        return pltpu.make_async_remote_copy(
            src_ref=send1.at[pl.ds(p * 4, 4)], dst_ref=recvC.at[pl.ds(a * 4, 4)], send_sem=c1_send.at[a],
            recv_sem=c1_recv.at[a], device_id={"ctx": sibling}, device_id_type=MESH)

    def to_owner(t):
        return pltpu.make_async_remote_copy(
            src_ref=send2.at[t], dst_ref=recv2.at[chip], send_sem=s2_sem.at[t], recv_sem=r2_sem.at[chip],
            device_id={"ctx": 2 * t + core}, device_id_type=MESH)

    def from_chip(t):
        return pltpu.make_async_remote_copy(
            src_ref=send2.at[t], dst_ref=recv2.at[t], send_sem=s2_sem.at[t], recv_sem=r2_sem.at[t],
            device_id={"ctx": 2 * t + core}, device_id_type=MESH)

    def to_chip(t):
        return pltpu.make_async_remote_copy(
            src_ref=send3.at[t], dst_ref=recv3.at[chip], send_sem=s3_sem.at[t], recv_sem=r3_sem.at[chip],
            device_id={"ctx": 2 * t + core}, device_id_type=MESH)

    def from_owner(t):
        return pltpu.make_async_remote_copy(
            src_ref=send3.at[t], dst_ref=recv3.at[t], send_sem=s3_sem.at[t], recv_sem=r3_sem.at[t],
            device_id={"ctx": 2 * t + core}, device_id_type=MESH)

    def entries_out(p, a):
        return pltpu.make_async_remote_copy(
            src_ref=sendS.at[pl.ds(a * 4, 4)], dst_ref=entry.at[pl.ds(p * 4, 4)], send_sem=c4_send.at[a],
            recv_sem=c4_recv.at[a], device_id={"ctx": sibling}, device_id_type=MESH)

    def both(p, a, j, which):
        mine = send1[p * 4 + j, which]
        other = recvC[a * 4 + j, which]
        return jnp.where(core == 0, mine, other), jnp.where(core == 0, other, mine)

    def join(p, a):
        to_sibling(p, a).wait_recv()
        for j in range(4):
            t = a * 4 + j
            p0, p1 = both(p, a, j, 0)
            l0, l1 = both(p, a, j, 1)
            b0, b1 = both(p, a, j, 2)
            send2[t, 0] = p0 * p1
            send2[t, 1] = l0 * p1 + l1
            send2[t, 2] = b0 + p0 * b1

            @pl.when(t != chip)
            def _():
                to_owner(t).start()

            @pl.when(t == chip)
            def _():
                recv2[t] = send2[t]

    def own_scan():
        for d in range(1, CHIPS):
            from_chip(lax.rem(chip + d, CHIPS)).wait_recv()
        state = jnp.zeros((SEG, LANES), F32)
        grad = state
        for c in range(CHIPS):
            send3[c, 0] = state
            state = state * recv2[c, 0] + recv2[c, 1]
        for c in reversed(range(CHIPS)):
            send3[c, 1] = grad
            grad = grad * recv2[c, 0] + recv2[c, 2]
        for d in sorted(range(1, CHIPS), key=lambda d: min(d, CHIPS - d)):
            to_chip(lax.rem(chip + d, CHIPS)).start()
        recv3[chip] = send3[chip]

    def split(p, a):
        for j in range(4):
            t = a * 4 + j

            @pl.when(t != chip)
            def _():
                from_owner(t).wait_recv()

            s0 = recv3[t, 0]
            g1 = recv3[t, 1]
            p0, p1 = both(p, a, j, 0)
            l0, _ = both(p, a, j, 1)
            _, b1 = both(p, a, j, 2)
            s1 = s0 * p0 + l0
            g0 = g1 * p1 + b1
            entry[p * 4 + j, 0] = jnp.where(core == 0, s0, s1)
            entry[p * 4 + j, 1] = jnp.where(core == 0, g0, g1)
            sendS[t, 0] = jnp.where(core == 0, s1, s0)
            sendS[t, 1] = jnp.where(core == 0, g1, g0)
        entries_out(p, a).start()

    def first_pass(it, _):
        p = first_order(it)
        for which in range(3):
            in_copy(p, which).wait()
        for c in range(2):
            lanes = pl.ds(c * LANES, LANES)
            x32[c] = xV[p, :, lanes].astype(F32)
            g32[c] = gV[p, :, lanes].astype(F32)
            r32[c] = rV[p, :, lanes]
        base = p * (2 * LEN)
        for i in range(LEN):
            for c in range(2):
                at = base + 2 * i + c
                rate = r32[c, pl.ds(i, SEG, stride=LEN), :]
                xv = x32[c, pl.ds(i, SEG, stride=LEN), :]
                gv = g32[c, pl.ds(i, SEG, stride=LEN), :]
                inv = 1.0 / (1.0 + rate * knT[i])
                step = rate * inv
                stepP[at] = step
                invP[at] = inv
                uP[at] = step * xv
                xP[at] = xv
                gP[at] = gv

        def n_group(ng, _):
            n0 = ng * 4
            prod = [None] * 8
            end = [None] * 8
            back = [None] * 8
            for i in range(LEN):
                step = [stepP[base + 2 * i + c] for c in range(2)]
                u = [uP[base + 2 * i + c] for c in range(2)]
                gv = [gP[base + 2 * i + c] for c in range(2)]
                for a in range(4):
                    kk = kT[i * N + n0 + a]
                    k2 = k2T[i * N + n0 + a]
                    qq = qT[i * N + n0 + a]
                    for c in range(2):
                        j = 2 * a + c
                        dec = 1.0 - step[c] * k2
                        decS[(p * LEN + i) * (2 * N) + 2 * n0 + j] = dec
                        emit = gv[c] * qq
                        drive = u[c] * kk
                        if i == 0:
                            prod[j] = dec
                            end[j] = drive
                            back[j] = emit * dec
                        else:
                            prod[j] = prod[j] * dec
                            end[j] = end[j] * dec + drive
                            back[j] = back[j] + emit * prod[j]
            for a in range(4):
                for c in range(2):
                    at = pl.multiple_of((c * N + n0 + a) * SEG, SEG)
                    sumP[pl.ds(at, SEG), :] = prod[2 * a + c]
                    sumL[pl.ds(at, SEG), :] = end[2 * a + c]
                    sumB[pl.ds(at, SEG), :] = back[2 * a + c]
            return 0

        lax.fori_loop(0, N // 4, n_group, 0)

        for j in range(4):
            o = p * 4 + j
            tile = j * 8 * SEG
            run_p = jnp.ones((SEG, LANES), F32)
            run_l = jnp.zeros((SEG, LANES), F32)
            ps, bs = [], []
            for s in range(SEG):
                pv = sumP[pl.ds(tile + s, SEG, stride=SEG), :]
                lv = sumL[pl.ds(tile + s, SEG, stride=SEG), :]
                ps.append(pv)
                bs.append(sumB[pl.ds(tile + s, SEG, stride=SEG), :])
                preP[o * SEG + s] = run_p
                preL[o * SEG + s] = run_l
                run_l = run_l * pv + lv
                run_p = run_p * pv
            send1[o, 0] = run_p
            send1[o, 1] = run_l
            run_p = jnp.ones((SEG, LANES), F32)
            run_b = jnp.zeros((SEG, LANES), F32)
            for s in reversed(range(SEG)):
                postP[o * SEG + s] = run_p
                postB[o * SEG + s] = run_b
                run_b = run_b * ps[s] + bs[s]
                run_p = run_p * ps[s]
            send1[o, 2] = run_b

        a = lax.rem(near + 1 + it, 2)

        @pl.when(it == 1)
        def _():
            pl.semaphore_wait(barrier, CHIPS + heads - 1)
            for b in range(2):
                to_sibling(2 * (1 - core) + b, b).start()

        @pl.when(it >= 2)
        def _():
            join(p, a)
        return 0

    lax.fori_loop(0, PAIRS, first_pass, 0)

    zero = jnp.zeros((SEG, LANES), F32)

    def clear(i, _):
        for n in range(N):
            accQ[i * N + n] = zero
            accK[i * N + n] = zero
        accN[i] = zero
        return 0

    lax.fori_loop(0, LEN, clear, 0)

    own_scan()

    def fill(at, _):
        i = lax.rem(at, LEN)
        u = [uP[2 * at + c] for c in range(2)]
        gv = [gP[2 * at + c] for c in range(2)]
        for n in range(N):
            kk = kT[i * N + n]
            qq = qT[i * N + n]
            for c in range(2):
                driveS[at * (2 * N) + 2 * n + c] = u[c] * kk
                emitS[at * (2 * N) + 2 * n + c] = gv[c] * qq
        return 0

    lax.fori_loop(0, PAIRS * LEN, fill, 0)

    def pair_at(it):
        return 2 * lax.rem(core + it // 2, 2) + lax.rem(near + it, 2)

    def part_lanes(p, c):
        return (pl.ds(0, WIDE), p * WIDE, WIDE) if c is None else (
            pl.ds(pl.multiple_of(c * LANES, LANES), LANES), p * WIDE + c * LANES, LANES)

    def head_copy(slot, p, c, h, owner):
        lanes, column, width = part_lanes(p, c)
        return pltpu.make_async_remote_copy(
            src_ref=sendB.at[p, :, pl.ds(pl.multiple_of(h * rows_out, rows_out), rows_out), lanes],
            dst_ref=o_ref.at[:, :, pl.ds(pl.multiple_of(owner * (PAIRS * WIDE) + column, width), width)],
            send_sem=h_send.at[slot, h], recv_sem=h_recv.at[slot, owner],
            device_id={"head": h}, device_id_type=MESH)

    def own_copy(slot, p, c):
        lanes, column, width = part_lanes(p, c)
        return pltpu.make_async_copy(
            sendB.at[p, :, pl.ds(pl.multiple_of(hd * rows_out, rows_out), rows_out), lanes],
            o_ref.at[:, :, pl.ds(pl.multiple_of(hd * (PAIRS * WIDE) + column, width), width)],
            own_sem.at[slot])

    def ship(slot, p, c):
        for d in sorted(range(1, heads), key=lambda d: -min(d, heads - d)):
            head_copy(slot, p, c, lax.rem(hd + d, heads), hd).start()
        own_copy(slot, p, c).start()

    def shipped(slot, p, c):
        own_copy(slot, p, c).wait()
        for d in range(1, heads):
            h = lax.rem(hd + d, heads)
            copy = head_copy(slot, p, c, h, h)
            copy.wait_send()
            copy.wait_recv()

    def second_pass(it):
        a = lax.rem(near + it, 2)
        p = 2 * lax.rem(core + it // 2, 2) + a
        base = p * (2 * LEN)

        @pl.when(it < 2)
        def _():
            split(p, a)

        @pl.when(it >= 2)
        def _():
            entries_out(p, a).wait_recv()

        for j in range(4):
            o = p * 4 + j
            s0 = entry[o, 0]
            g0 = entry[o, 1]
            tile = j * 8 * SEG
            for s in range(SEG):
                at = o * SEG + s
                sIn[pl.ds(tile + s, SEG, stride=SEG), :] = preP[at] * s0 + preL[at]
                gIn[pl.ds(tile + s, SEG, stride=SEG), :] = postP[at] * g0 + postB[at]

        return p, base

    def grads_of(p, base, chunks):
        width = len(chunks)

        def forward(i, states):
            states = list(states)
            gv = [gP[base + 2 * i + c] for c in chunks]
            for n in range(N):
                kk = kT[i * N + n]
                total = accQ[i * N + n]
                for b, c in enumerate(chunks):
                    j = n * width + b
                    kpS[i * (2 * N) + j] = kk * states[j]
                    states[j] = decS[(p * LEN + i) * (2 * N) + 2 * n + c] * states[j] + driveS[(p * LEN + i) * (2 * N) + 2 * n + c]
                    total = total + gv[b] * states[j]
                accQ[i * N + n] = total
            return tuple(states)

        def forward_some(b, states):
            for r in range(STEPS):
                states = forward(b * STEPS + r, states)
            return states

        def start(ref):
            return tuple(
                ref[pl.ds(pl.multiple_of((c * N + n) * SEG, SEG), SEG), :] for n in range(N) for c in chunks)

        lax.fori_loop(0, LEN // STEPS, forward_some, start(sIn))

        def backward(it2, grads):
            i = LEN - 1 - it2
            grads = list(grads)
            step = [stepP[base + 2 * i + c] for c in chunks]
            twice = [s + s for s in step]
            u = [uP[base + 2 * i + c] for c in chunks]
            key_dot = [None] * width
            weighted = [None] * width
            for n in range(N):
                kk = kT[i * N + n]
                total = accK[i * N + n]
                for b, c in enumerate(chunks):
                    j = n * width + b
                    kprev = kpS[i * (2 * N) + j]
                    grad = grads[j] + emitS[(p * LEN + i) * (2 * N) + 2 * n + c]
                    gk = grad * kk
                    wk = gk * kprev
                    key_dot[b] = gk if n == 0 else key_dot[b] + gk
                    weighted[b] = wk if n == 0 else weighted[b] + wk
                    total = total + grad * (u[b] - twice[b] * kprev)
                    grads[j] = grad * decS[(p * LEN + i) * (2 * N) + 2 * n + c]
                accK[i * N + n] = total
            norm_sum = accN[i]
            for b, c in enumerate(chunks):
                at = base + 2 * i + c
                inv = invP[at]
                outI[b, pl.ds(i, SEG, stride=LEN), :] = step[b] * key_dot[b]
                grad_step = xP[at] * key_dot[b] - weighted[b]
                outR[b, pl.ds(i, SEG, stride=LEN), :] = grad_step * (inv * inv)
                norm_sum = norm_sum + grad_step * (step[b] * step[b])
            accN[i] = norm_sum
            return tuple(grads)

        def backward_some(b, grads):
            for r in range(STEPS):
                grads = backward(b * STEPS + r, grads)
            return grads

        lax.fori_loop(0, LEN // STEPS, backward_some, start(gIn))
        for b, c in enumerate(chunks):
            lanes = pl.ds(c * LANES, LANES) if isinstance(c, int) else pl.ds(pl.multiple_of(c * LANES, LANES), LANES)
            sendB[p, 0, :, lanes] = outI[b].astype(BF16)
            sendB[p, 1, :, lanes] = outR[b].astype(BF16)

    def pair_grads(it, _):
        p, base = second_pass(it)
        grads_of(p, base, (0, 1))
        ship(it, p, None)
        return 0

    lax.fori_loop(0, PAIRS, pair_grads, 0)

    ones = jnp.ones((2 * LANES, LANES), BF16)
    lane = lax.broadcasted_iota(jnp.int32, (TOKENS, LANES), 1)

    def lane_sums(parts):
        whole = jnp.concatenate(parts, axis=0)
        high = whole.astype(BF16)
        low = (whole - high.astype(F32)).astype(BF16)
        return jnp.dot(jnp.concatenate([high, low], axis=1), ones, preferred_element_type=F32)

    merged = lane_sums([accN[i] for i in range(LEN)]) * (-2.0 * kL[...])
    for n in range(N):
        merged = jnp.where(lane == n, merged + lane_sums([accK[i * N + n] for i in range(LEN)]), merged)
        merged = jnp.where(lane == N + n, lane_sums([accQ[i * N + n] for i in range(LEN)]), merged)
    for i in range(LEN):
        sums[pl.ds(i, SEG, stride=LEN), :] = merged[i * SEG:(i + 1) * SEG]

    turned = sums[...].T
    quarter = lax.broadcasted_iota(jnp.int32, (SEG, LANES), 1) // rows_out
    for h in range(heads):
        packed = zero
        for q in range(2 * N // SEG):
            moved = turned[q * SEG:(q + 1) * SEG]
            if q != h:
                moved = pltpu.roll(moved, (rows_out * (q - h)) % LANES, 1)
            packed = jnp.where(quarter == q, moved, packed)
        packS[h] = packed

    def sum_copy(h, src):
        return pltpu.make_async_remote_copy(
            src_ref=packS.at[h], dst_ref=rs_ref.at[src], send_sem=rs_send.at[h], recv_sem=rs_recv.at[src],
            device_id={"head": h}, device_id_type=MESH)

    for d in range(1, heads):
        sum_copy(lax.rem(hd + d, heads), hd).start()
    rs_ref[hd] = packS[hd]

    for d in range(1, CHIPS):
        to_owner(lax.rem(chip + d, CHIPS)).wait_send()
        to_chip(lax.rem(chip + d, CHIPS)).wait_send()
    for a in range(2):
        to_sibling(a, a).wait_send()
        entries_out(a, a).wait_send()
    for it in range(PAIRS):
        shipped(it, pair_at(it), None)
    for d in range(1, heads):
        h = lax.rem(hd + d, heads)
        copy = sum_copy(h, h)
        copy.wait_send()
        copy.wait_recv()


def finish(heads, b_ref, s_ref, oi_ref, or_ref, ok_ref, oq_ref, small, sem):
    first = pltpu.make_async_copy(b_ref.at[pl.ds(0, 1)], oi_ref, sem.at[0])
    second = pltpu.make_async_copy(b_ref.at[pl.ds(1, 1)], or_ref, sem.at[1])
    first.start()
    second.start()
    total = s_ref[0]
    for h in range(1, heads):
        total = total + s_ref[h]
    rows_out = TOKENS // heads
    for q in range(2 * N // SEG):
        small[q // 2, (q % 2) * SEG:(q % 2 + 1) * SEG, :] = total[:, q * rows_out:(q + 1) * rows_out]
    third = pltpu.make_async_copy(small.at[0], ok_ref.at[0], sem.at[2])
    fourth = pltpu.make_async_copy(small.at[1], oq_ref.at[0], sem.at[3])
    third.start()
    fourth.start()
    for copy in (first, second, third, fourth):
        copy.wait()


def shards(heads):
    def run(inputs, step_rate, key_rows, query_rows, grad_out):
        rows_out = TOKENS // heads
        width = heads * PAIRS * WIDE
        vmem = pl.BlockSpec(memory_space=pltpu.VMEM)
        hbm = pl.BlockSpec(memory_space=pltpu.HBM)
        tile = (SEG, LANES)

        def regs(*lead):
            return pltpu.VMEM(lead + tile, F32)

        dma = pltpu.SemaphoreType.DMA
        wide = jax.ShapeDtypeStruct((1, rows_out, width), BF16)
        small = jax.ShapeDtypeStruct((1, N, rows_out), F32)
        grads, partial = pl.pallas_call(
            lambda *refs: kernel(heads, *refs),
            out_shape=(
                pltpu.VMEM((2, rows_out, width), BF16),
                pltpu.VMEM((heads, SEG, LANES), F32),
            ),
            in_specs=[hbm] * 5,
            out_specs=(vmem, vmem),
            scratch_shapes=[
                pltpu.VMEM((PAIRS, TOKENS, WIDE), BF16), pltpu.VMEM((PAIRS, TOKENS, WIDE), F32),
                pltpu.VMEM((PAIRS, TOKENS, WIDE), BF16),
                pltpu.VMEM((N, TOKENS), BF16), pltpu.VMEM((N, TOKENS), BF16),
                regs(LEN * N), regs(LEN * N), regs(LEN * N), regs(LEN), pltpu.VMEM((TOKENS, LANES), F32),
                *[pltpu.VMEM((2, TOKENS, LANES), F32) for _ in range(3)],
                *[regs(PAIRS * 2 * LEN) for _ in range(5)],
                regs(PAIRS * LEN * 2 * N),
                regs(PAIRS * LEN * 2 * N),
                regs(PAIRS * LEN * 2 * N),
                *[pltpu.VMEM((2 * N * SEG, LANES), F32) for _ in range(3)],
                *[regs(CTX * SEG) for _ in range(4)],
                regs(CTX, 3), regs(CHIPS, 3), regs(CHIPS, 3), regs(CHIPS, 3),
                regs(CHIPS, 2), regs(CHIPS, 2), regs(CHIPS, 2), regs(CTX, 2),
                pltpu.VMEM((2 * N * SEG, LANES), F32), pltpu.VMEM((2 * N * SEG, LANES), F32),
                regs(LEN * 2 * N),
                regs(LEN * N), regs(LEN * N), regs(LEN),
                pltpu.VMEM((2, TOKENS, LANES), F32), pltpu.VMEM((2, TOKENS, LANES), F32),
                pltpu.VMEM((PAIRS, 2, TOKENS, WIDE), BF16),
                pltpu.VMEM((TOKENS, LANES), F32), regs(heads),
                dma((3 * PAIRS + 2,)),
                dma((2,)), dma((2,)), *[dma((CHIPS,)) for _ in range(4)], dma((2,)), dma((2,)),
                dma((PAIRS, heads)), dma((PAIRS, heads)), dma((PAIRS,)), dma((heads,)), dma((heads,)),
            ],
            compiler_params=pltpu.CompilerParams(
                collective_id=0, has_side_effects=True, vmem_limit_bytes=48 * 1024 * 1024),
        )(*(
            pltpu.with_memory_space_constraint(a, pltpu.HBM)
            for a in (inputs, step_rate, jnp.swapaxes(key_rows, 1, 2), jnp.swapaxes(query_rows, 1, 2), grad_out)
        ))
        grads_in, grads_rate, keys, queries = pl.pallas_call(
            lambda *refs: finish(heads, *refs),
            out_shape=(wide, wide, small, small),
            in_specs=[vmem, vmem],
            out_specs=(hbm, hbm, hbm, hbm),
            scratch_shapes=[pltpu.VMEM((2, N, rows_out), F32), dma((4,))],
        )(*(pltpu.with_memory_space_constraint(a, pltpu.VMEM) for a in (grads, partial)))
        return grads_in, grads_rate, jnp.swapaxes(keys, 1, 2), jnp.swapaxes(queries, 1, 2)

    return run


def solution(mesh):
    placed = (
        P("dp", "ctx", "head"),
        P("dp", "ctx", "head"),
        P("dp", "ctx", None),
        P("dp", "ctx", None),
        P("dp", "ctx", "head"),
    )
    out = P("dp", ("ctx", "head"), None)
    return jax.shard_map(
        shards(mesh.shape["head"]),
        mesh=mesh,
        in_specs=placed,
        out_specs=(out, out, out, out),
        check_vma=False,
    )
```
